256 devices in a mesh: seq: 32 (over x, y, z_lo), chan: 8 (over z_hi, core).
Axes of the slice: x: 4, y: 4, z: 8 (z_hi: 4, z_lo: 2; z = z_hi * 2 + z_lo), core: 2. Of those that a mesh axis runs over, the one named last changes fastest.
Arguments:
- value: bfloat16 [32768, 2048], P('seq', 'chan'), may hold values from -6 to 6
- gate_in: bfloat16 [32768, 2048], P('seq', 'chan'), may hold values from -6 to 6
- gate_out: bfloat16 [32768, 2048], P('seq', 'chan'), may hold values from -6 to 6
- skip_weight: float32 [2048], P('chan'), may hold values from -1 to 1
- spectrum: float32 [2, 512, 128, 2048], P(None, 'seq', None, 'chan'), may hold values from -6 to 6
- out_weight: bfloat16 [2048, 2048], P('chan'), may hold values from -0.125 to 0.125
Outputs:
- projected: bfloat16 [32768, 2048], P(('seq', 'chan'))
The draws below stay inside these ranges and needn't reach their ends.
All inputs are finite; a program needn't handle non-finite values.
Results may differ from the reference program's by a relative error of at most 0.0057.
Values may be sent and summed in bfloat16 or wider, within the bound.
A program may use at most 128 MiB of HBM per device.

```python
import math
import jax
import jax.numpy as jnp
from jax import lax

COLS = 128
CHANNELS = 2048
FEATURES = 2048
SEQ_LEN = 32768
PADDED = 65536
ROWS = 512


def block_scale(key, extent, cuts, smallest, largest):
    def one(dim, shards_of):
        heights = jax.random.uniform(jax.random.fold_in(jax.random.fold_in(key, 6), dim), (shards_of,), jnp.float32, smallest / len(cuts), largest / len(cuts))
        return jnp.repeat(jnp.exp(heights), extent[dim] // shards_of).reshape((-1,) + (1,) * (len(extent) - dim - 1))

    loudness = one(*cuts[0])
    for cut in cuts[1:]:
        loudness = loudness * one(*cut)
    return loudness


def bell_draw(rng, shape, spread, bound, pieces=(), kind=jnp.bfloat16):
    level = block_scale(rng, shape, pieces, -0.22, 0.18) if pieces else 1.0
    entries = jax.random.normal(rng, shape, jnp.float32) * spread * level
    return jnp.minimum(jnp.maximum(entries, -bound), bound).astype(kind)


def setup_inputs(seed: int = 0) -> dict:
    keys = jax.random.split(jax.random.key(seed), 7)
    value = bell_draw(keys[0], (SEQ_LEN, CHANNELS), 1.0, 6.0, ((0, 32), (1, 8)))
    gate_in = bell_draw(keys[1], (SEQ_LEN, CHANNELS), 1.0, 6.0, ((0, 32), (1, 8)))
    gate_out = bell_draw(keys[2], (SEQ_LEN, CHANNELS), 1.0, 6.0, ((0, 32), (1, 8)))
    skip_weight = jnp.clip(jax.random.uniform(keys[3], (CHANNELS,), jnp.float32, -1.0, 1.0) * block_scale(keys[3], (CHANNELS,), ((0, 8),), -0.4, 0.0), -1.0, 1.0)
    spectrum = bell_draw(keys[4], (2, ROWS, COLS, CHANNELS), 1.0, 6.0, ((1, 32), (3, 8)), jnp.float32)
    out_weight = bell_draw(keys[5], (CHANNELS, FEATURES), CHANNELS ** -0.5, 0.125, ((0, 8),))
    return dict(value=value, gate_in=gate_in, gate_out=gate_out, skip_weight=skip_weight, spectrum=spectrum, out_weight=out_weight)


def reference(value, gate_in, gate_out, skip_weight, spectrum, out_weight):
    mixed = (gate_in.astype(jnp.float32) * value.astype(jnp.float32)).astype(jnp.bfloat16)
    block_width = math.gcd(CHANNELS, 128)
    block_count = CHANNELS // block_width
    mixed_blocks = mixed.reshape(SEQ_LEN, block_count, block_width).transpose(1, 0, 2)
    spectra = spectrum.reshape(2, ROWS, COLS, block_count, block_width)
    spectra = spectra.transpose(3, 0, 2, 1, 4).reshape(block_count, 2, PADDED, block_width)

    def convolve(pair):
        signal, filt = pair
        padded_input = jnp.concatenate(
            [signal.astype(jnp.float32), jnp.zeros((SEQ_LEN, block_width), jnp.float32)], axis=0)
        freq = jnp.fft.fft(padded_input, axis=0)
        filtered = freq * lax.complex(filt[0], filt[1])
        result = jnp.real(jnp.fft.ifft(filtered, axis=0))[:SEQ_LEN]
        return result.astype(jnp.float32)

    long_conv = lax.map(convolve, (mixed_blocks, spectra))
    long_conv = long_conv.transpose(1, 0, 2).reshape(SEQ_LEN, CHANNELS)
    inner = long_conv + skip_weight[None, :] * mixed.astype(jnp.float32)
    gated = (gate_out.astype(jnp.float32) * inner).astype(jnp.bfloat16)
    return jnp.dot(gated, out_weight, preferred_element_type=jnp.float32).astype(jnp.bfloat16)
```

```python
import functools
import math

import jax
import jax.numpy as jnp
import ml_dtypes
import numpy as np
from jax import lax
from jax.experimental import pallas as pl
from jax.experimental.pallas import tpu as pltpu
from jax.sharding import PartitionSpec as P

COLS = 128
LANE = 128
CH = 8
BAND = 16
GROUP = 8
MESH = pl.DeviceIdType.MESH
F32 = jnp.float32
BF16 = jnp.bfloat16


def two_terms(matrix):
    high = matrix.astype(np.float32).astype(ml_dtypes.bfloat16)
    low = (matrix - high.astype(np.float64)).astype(np.float32).astype(ml_dtypes.bfloat16)
    return np.stack([high, low])


def constants(seq_size):
    half_rows = 8 * seq_size
    row_count = 2 * half_rows
    padded_len = row_count * COLS
    k1 = np.arange(row_count)
    a = np.arange(half_rows)
    b = np.arange(COLS)
    row = 2.0 * np.pi / row_count * (np.outer(k1, a) % row_count)
    fwd_row = np.concatenate([np.cos(row), -np.sin(row)], axis=0)
    twist = 2.0 * np.pi / padded_len * (np.outer(k1, b) % padded_len)
    turn = np.stack([np.cos(twist), np.sin(twist)]).astype(np.float32)
    col = 2.0 * np.pi / COLS * (np.outer(b, b) % COLS)
    cos, sin = np.cos(col), np.sin(col)
    fwd_col = np.block([[cos, -sin], [sin, cos]])
    inv_col = np.block([[cos, sin], [-sin, cos]])
    groups = seq_size // min(GROUP, seq_size)
    back = row.T.reshape(half_rows, groups, -1)
    inv_row = np.concatenate([np.cos(back), -np.sin(back)], axis=2) / padded_len
    inv_row = np.ascontiguousarray(inv_row.transpose(1, 0, 2))
    return two_terms(fwd_row), turn, two_terms(fwd_col), two_terms(inv_col), two_terms(inv_row)


def mm(x, y):
    return jnp.dot(x, y, preferred_element_type=F32)


def conv_kernel(
    seq_size,
    chan_size,
    value,
    gate_in,
    gate_out,
    skip,
    spectrum,
    fwd_row_hbm,
    turn_hbm,
    fwd_col_hbm,
    inv_col_hbm,
    inv_row_hbm,
    out,
    fwd_row,
    turn,
    fwd_col,
    inv_col,
    inv_row,
    gate_buf,
    spec_buf,
    xsend,
    xrecv,
    xwide,
    xgrid,
    hwide,
    hsend,
    hrecv,
    freq,
    back,
    total,
    ysend,
    yrecv,
    ywide,
    gate_t,
    gsend,
    load_sem,
    spec_sem,
    xs,
    xr,
    hs,
    hr,
    ys,
    yr,
    gs,
    gr,
):
    me = lax.axis_index("seq")
    mc = lax.axis_index("chan")
    half_rows = 8 * seq_size
    width = CH * seq_size
    members = min(GROUP, seq_size)
    groups = seq_size // members
    krows = members * BAND

    loads = [
        pltpu.make_async_copy(fwd_row_hbm, fwd_row, load_sem.at[0]),
        pltpu.make_async_copy(turn_hbm, turn, load_sem.at[1]),
        pltpu.make_async_copy(fwd_col_hbm, fwd_col, load_sem.at[2]),
        pltpu.make_async_copy(inv_col_hbm, inv_col, load_sem.at[3]),
        pltpu.make_async_copy(inv_row_hbm, inv_row, load_sem.at[4]),
        pltpu.make_async_copy(gate_out, gate_buf, load_sem.at[5]),
    ]
    spec_loads = [
        pltpu.make_async_copy(spectrum.at[part], spec_buf.at[part], spec_sem.at[part])
        for part in range(2)
    ]
    for copy in spec_loads + loads:
        copy.start()

    barrier = pltpu.get_barrier_semaphore()

    def greet_seq(d, _):
        peer = lax.rem(me + d, seq_size)
        pl.semaphore_signal(barrier, inc=1, device_id=(peer, mc), device_id_type=MESH)
        return 0

    def greet_chan(d, _):
        peer = lax.rem(mc + d, chan_size)
        pl.semaphore_signal(barrier, inc=1, device_id=(me, peer), device_id_type=MESH)
        return 0

    lax.fori_loop(1, seq_size, greet_seq, 0)
    lax.fori_loop(1, chan_size, greet_chan, 0)

    def exchange(src_of, dst, send_sem, recv_sem):
        own = pltpu.make_async_copy(src_of(me), dst, recv_sem)
        own.start()

        def send(d, _):
            peer = lax.rem(me + d, seq_size)
            pltpu.make_async_remote_copy(
                src_ref=src_of(peer),
                dst_ref=dst,
                send_sem=send_sem,
                recv_sem=recv_sem,
                device_id=(peer, mc),
                device_id_type=MESH,
            ).start()
            return 0

        lax.fori_loop(1, seq_size, send, 0)

    for pair in range(4):
        halves = []
        for a in (2 * pair, 2 * pair + 1):
            rows = slice(a * COLS, (a + 1) * COLS)
            mixed = (gate_in[rows, :].astype(F32) * value[rows, :].astype(F32)).astype(BF16)
            halves.append(mixed.astype(F32).T.reshape(seq_size, CH, LANE))
        xsend[:, pair * 16 : (pair + 1) * 16, :] = jnp.concatenate(halves, axis=1).astype(BF16)

    pl.semaphore_wait(barrier, seq_size - 1 + chan_size - 1)
    exchange(lambda peer: xsend.at[peer], xrecv.at[me], xs, xr)

    for part in range(2):
        spec_loads[part].wait()

        def turn_row(k, _):
            start = pl.multiple_of(k * width, width)
            hwide[pl.ds(start, width), :] = spec_buf[part, k].T
            return 0

        lax.fori_loop(0, BAND, turn_row, 0)

        def pack(dest, _):
            for c in range(CH):
                rows = hwide[pl.ds(dest * CH + c, BAND, stride=width), :]
                hsend[part, dest, c * BAND : (c + 1) * BAND, :] = rows.astype(BF16)
            return 0

        lax.fori_loop(0, seq_size, pack, 0)
        exchange(
            lambda peer: hsend.at[part, peer],
            hrecv.at[part, me],
            hs.at[part],
            hr.at[part, me // members],
        )

    loads[5].wait()
    for a in range(8):
        gate_t[a] = gate_buf[a * COLS : (a + 1) * COLS, :].astype(F32).T.astype(BF16)

    for copy in loads[:5]:
        copy.wait()
    pltpu.make_async_copy(xsend, xrecv, xr).wait()
    xwide[...] = xrecv[...].astype(F32).reshape(seq_size * 64, LANE)
    for c in range(CH):
        xgrid[:, c * LANE : (c + 1) * LANE] = xwide[pl.ds(c, half_rows, stride=CH), :].astype(BF16)

    row_count = 2 * half_rows

    def forward(g, _):
        rows = pl.ds(pl.multiple_of(g * krows, krows), krows)
        rows_im = pl.ds(pl.multiple_of(row_count + g * krows, krows), krows)
        cos, sin = turn[0, rows, :], turn[1, rows, :]
        for pair in range(CH // 2):
            x = xgrid[:, pair * 256 : (pair + 1) * 256]
            re = mm(fwd_row[0, rows, :], x) + mm(fwd_row[1, rows, :], x)
            im = mm(fwd_row[0, rows_im, :], x) + mm(fwd_row[1, rows_im, :], x)
            for h in range(2):
                r = re[:, h * LANE : (h + 1) * LANE]
                i = im[:, h * LANE : (h + 1) * LANE]
                turned = jnp.concatenate([r * cos + i * sin, i * cos - r * sin], axis=1)
                high = turned.astype(BF16)
                low = (turned - high.astype(F32)).astype(BF16)
                freq[2 * pair + h, rows, :] = (
                    mm(high, fwd_col[0]) + mm(high, fwd_col[1]) + mm(low, fwd_col[0])
                )
        return 0

    lax.fori_loop(0, groups, forward, 0)

    total[...] = jnp.zeros_like(total)
    def inverse(g, _):
        members_at = pl.ds(pl.multiple_of(g * members, members), members)
        for part in range(2):
            block = hrecv.at[part, members_at]
            pltpu.make_async_copy(hsend.at[part, members_at], block, hr.at[part, g]).wait()
        rows = pl.ds(pl.multiple_of(g * krows, krows), krows)
        cos, sin = turn[0, rows, :], turn[1, rows, :]
        for c in range(CH):
            band = slice(c * BAND, (c + 1) * BAND)
            h_re = hrecv[0, members_at, band, :].astype(F32).reshape(krows, LANE)
            h_im = hrecv[1, members_at, band, :].astype(F32).reshape(krows, LANE)
            f_re, f_im = freq[c, rows, :LANE], freq[c, rows, LANE:]
            prod = jnp.concatenate([f_re * h_re - f_im * h_im, f_re * h_im + f_im * h_re], axis=1)
            prod = prod.astype(BF16)
            grid = mm(prod, inv_col[0]) + mm(prod, inv_col[1])
            b_re, b_im = grid[:, :LANE], grid[:, LANE:]
            lanes = slice(c * LANE, (c + 1) * LANE)
            back[:krows, lanes] = (b_re * cos - b_im * sin).astype(BF16)
            back[krows:, lanes] = (b_re * sin + b_im * cos).astype(BF16)
        for pair in range(CH // 2):
            lanes = slice(pair * 256, (pair + 1) * 256)
            total[:, lanes] += mm(inv_row[0, g], back[:, lanes]) + mm(inv_row[1, g], back[:, lanes])
        return 0

    lax.fori_loop(0, groups, inverse, 0)

    weights = skip[me]
    for pair in range(CH // 2):
        halves = []
        for c in (2 * pair, 2 * pair + 1):
            lanes = slice(c * LANE, (c + 1) * LANE)
            inner = total[:, lanes] + weights[c : c + 1, :] * xgrid[:, lanes].astype(F32)
            halves.append(inner.reshape(seq_size, 8, LANE))
        ysend[:, pair * 16 : (pair + 1) * 16, :] = jnp.concatenate(halves, axis=1).astype(BF16)
    exchange(lambda peer: ysend.at[peer], yrecv.at[me], ys, yr)
    pltpu.make_async_copy(ysend, yrecv, yr).wait()
    ywide[...] = yrecv[...].astype(F32).reshape(seq_size * 64, LANE)
    for a in range(8):
        inner = ywide[pl.ds(a, width, stride=8), :]
        gsend[a] = (gate_t[a].astype(F32) * inner).astype(BF16)

    own = pltpu.make_async_copy(gsend.at[mc], out.at[mc], gr)
    own.start()

    def send(d, _):
        peer = lax.rem(mc + d, chan_size)
        pltpu.make_async_remote_copy(
            src_ref=gsend.at[peer],
            dst_ref=out.at[mc],
            send_sem=gs,
            recv_sem=gr,
            device_id=(me, peer),
            device_id_type=MESH,
        ).start()
        return 0

    lax.fori_loop(1, chan_size, send, 0)
    pltpu.make_async_copy(gsend, out, gr).wait()

    others = pl.ds(0, seq_size - 1)
    pltpu.make_async_copy(xsend.at[others], xrecv.at[others], xs).wait()
    for part in range(2):
        pltpu.make_async_copy(hsend.at[part, others], hrecv.at[part, others], hs.at[part]).wait()
    pltpu.make_async_copy(ysend.at[others], yrecv.at[others], ys).wait()
    rest = pl.ds(0, chan_size - 1)
    pltpu.make_async_copy(gsend.at[rest], out.at[rest], gs).wait()


def long_conv(seq_size, chan_size, value, gate_in, gate_out, skip_weight, spectrum):
    half_rows = 8 * seq_size
    row_count = 2 * half_rows
    width = CH * seq_size
    members = min(GROUP, seq_size)
    groups = seq_size // members
    krows = members * BAND
    mats = constants(seq_size)
    skip = jnp.broadcast_to(skip_weight.reshape(seq_size, CH, 1), (seq_size, CH, LANE))
    vmem = pl.BlockSpec(memory_space=pltpu.VMEM)
    hbm = pl.BlockSpec(memory_space=pl.ANY)
    dma = pltpu.SemaphoreType.DMA
    return pl.pallas_call(
        functools.partial(conv_kernel, seq_size, chan_size),
        out_shape=jax.ShapeDtypeStruct((chan_size, width, LANE), BF16),
        in_specs=[vmem, vmem, hbm, vmem, hbm] + [hbm] * 5,
        out_specs=hbm,
        scratch_shapes=[
            *[pltpu.VMEM(m.shape, F32 if m.dtype == np.float32 else BF16) for m in mats],
            pltpu.VMEM((1024, width), BF16),
            pltpu.VMEM((2, BAND, COLS, width), F32),
            pltpu.VMEM((seq_size, 64, LANE), BF16),
            pltpu.VMEM((seq_size, 64, LANE), BF16),
            pltpu.VMEM((seq_size * 64, LANE), F32),
            pltpu.VMEM((half_rows, CH * LANE), BF16),
            pltpu.VMEM((BAND * width, LANE), F32),
            pltpu.VMEM((2, seq_size, CH * BAND, LANE), BF16),
            pltpu.VMEM((2, seq_size, CH * BAND, LANE), BF16),
            pltpu.VMEM((CH, row_count, 2 * LANE), F32),
            pltpu.VMEM((2 * krows, CH * LANE), BF16),
            pltpu.VMEM((half_rows, CH * LANE), F32),
            pltpu.VMEM((seq_size, 64, LANE), BF16),
            pltpu.VMEM((seq_size, 64, LANE), BF16),
            pltpu.VMEM((seq_size * 64, LANE), F32),
            pltpu.VMEM((8, width, LANE), BF16),
            pltpu.VMEM((8, width, LANE), BF16),
            dma((6,)),
            dma((2,)),
            dma,
            dma,
            dma((2,)),
            dma((2, groups)),
            dma,
            dma,
            dma,
            dma,
        ],
        compiler_params=pltpu.CompilerParams(
            collective_id=0, has_side_effects=True, vmem_limit_bytes=50 * 1024 * 1024
        ),
        name="long_conv",
    )(value, gate_in, gate_out, skip, spectrum, *[jnp.asarray(m) for m in mats])


def local(value, gate_in, gate_out, skip_weight, spectrum, out_weight):
    seq_size = lax.axis_size("seq")
    chan_size = lax.axis_size("chan")
    weight = lax.all_gather(out_weight, "chan", axis=0, tiled=True)
    gated = long_conv(seq_size, chan_size, value, gate_in, gate_out, skip_weight, spectrum)
    gated = gated.reshape(-1, LANE)
    out = lax.dot_general(gated, weight, (((0,), (0,)), ((), ())), preferred_element_type=F32)
    return out.astype(BF16)


def solution(mesh):
    placed = (
        P("seq", "chan"),
        P("seq", "chan"),
        P("seq", "chan"),
        P("chan"),
        P(None, "seq", None, "chan"),
        P("chan", None),
    )
    return jax.shard_map(
        local, mesh=mesh, in_specs=placed, out_specs=P(("seq", "chan"), None), check_vma=False
    )
```

```python
import functools
import math

import jax
import jax.numpy as jnp
import ml_dtypes
import numpy as np
from jax import lax
from jax.experimental import pallas as pl
from jax.experimental.pallas import tpu as pltpu
from jax.sharding import PartitionSpec as P

COLS = 128
LANE = 128
CH = 8
BAND = 16
GROUP = 8
NODES = 4
SPANS, SPAN = 4, 512
MESH = pl.DeviceIdType.MESH
F32 = jnp.float32
BF16 = jnp.bfloat16


def two_terms(matrix):
    high = matrix.astype(np.float32).astype(ml_dtypes.bfloat16)
    low = (matrix - high.astype(np.float64)).astype(np.float32).astype(ml_dtypes.bfloat16)
    return np.stack([high, low])


def constants(seq_size):
    half_rows = 8 * seq_size
    row_count = 2 * half_rows
    padded_len = row_count * COLS
    k1 = np.arange(row_count)
    a = np.arange(half_rows)
    b = np.arange(COLS)
    row = 2.0 * np.pi / row_count * (np.outer(k1, a) % row_count)
    fwd_row = np.concatenate([np.cos(row), -np.sin(row)], axis=0)
    twist = 2.0 * np.pi / padded_len * (np.outer(k1, b) % padded_len)
    turn = np.stack([np.cos(twist), np.sin(twist)]).astype(np.float32)
    col = 2.0 * np.pi / COLS * (np.outer(b, b) % COLS)
    cos, sin = np.cos(col), np.sin(col)
    fwd_col = np.block([[cos, -sin], [sin, cos]])
    inv_col = np.block([[cos, sin], [-sin, cos]])
    groups = seq_size // min(GROUP, seq_size)
    back = row.T.reshape(half_rows, groups, -1)
    inv_row = np.concatenate([np.cos(back), -np.sin(back)], axis=2) / padded_len
    inv_row = np.ascontiguousarray(inv_row.transpose(1, 0, 2))
    return two_terms(fwd_row), turn, two_terms(fwd_col), two_terms(inv_col), two_terms(inv_row)


def mm(x, y):
    return jnp.dot(x, y, preferred_element_type=F32)


def conv_kernel(
    seq_size,
    value_hbm,
    gate_in_hbm,
    gate_out_hbm,
    skip,
    spectrum,
    weight_hbm,
    fwd_row_hbm,
    turn_hbm,
    fwd_col_hbm,
    inv_col_hbm,
    inv_row_hbm,
    out,
    fwd_row,
    turn,
    fwd_col,
    inv_col,
    inv_row,
    value,
    gate_in,
    gate_out,
    spec_buf,
    weight,
    xsend,
    xrecv,
    xwide,
    xgrid,
    hwide,
    hsend,
    hrecv,
    freq,
    back,
    total,
    ysend,
    yrecv,
    ywide,
    gsend,
    grecv,
    partial,
    mate_part,
    load_sem,
    spec_sem,
    xs,
    xr,
    hs,
    hr,
    ys,
    yr,
    gs,
    gr,
    ws,
    wr,
    es,
    er,
    ms,
    mr,
):
    me = lax.axis_index("seq")
    mc = lax.axis_index("chan")
    half_rows = 8 * seq_size
    row_count = 2 * half_rows
    width = CH * seq_size
    members = GROUP
    groups = seq_size // members
    krows = members * BAND
    px, py, low = me // 8, lax.rem(me // 2, 4), lax.rem(me, 2)
    node, core = mc // 2, lax.rem(mc, 2)
    pair_chip = me + 1 - 2 * low
    near = lax.rem(node + 3 + 2 * low, NODES)
    far = lax.rem(node + 5 - 2 * low, NODES)
    across = lax.rem(node + 2, NODES)
    mine = lax.rem(px + py, 2)
    beside = [
        lax.rem(px + 1, 4) * 8 + py * 2 + low,
        lax.rem(px + 3, 4) * 8 + py * 2 + low,
        px * 8 + lax.rem(py + 1, 4) * 2 + low,
        px * 8 + lax.rem(py + 3, 4) * 2 + low,
    ]

    def remote(src, dst, send_sem, recv_sem, seq, chan):
        return pltpu.make_async_remote_copy(
            src_ref=src,
            dst_ref=dst,
            send_sem=send_sem,
            recv_sem=recv_sem,
            device_id=(seq, chan),
            device_id_type=MESH,
        )

    mixed_loads = [
        pltpu.make_async_copy(value_hbm, value, load_sem.at[6]),
        pltpu.make_async_copy(gate_in_hbm, gate_in, load_sem.at[7]),
    ]
    weight_load = pltpu.make_async_copy(weight_hbm, weight.at[node], load_sem.at[8])
    loads = [
        pltpu.make_async_copy(fwd_row_hbm, fwd_row, load_sem.at[0]),
        pltpu.make_async_copy(turn_hbm, turn, load_sem.at[1]),
        pltpu.make_async_copy(fwd_col_hbm, fwd_col, load_sem.at[2]),
        pltpu.make_async_copy(inv_col_hbm, inv_col, load_sem.at[3]),
        pltpu.make_async_copy(inv_row_hbm, inv_row, load_sem.at[4]),
        pltpu.make_async_copy(gate_out_hbm, gate_out, load_sem.at[5]),
    ]
    spec_loads = [
        pltpu.make_async_copy(spectrum.at[part], spec_buf.at[part], spec_sem.at[part])
        for part in range(2)
    ]
    for copy in mixed_loads + [weight_load] + spec_loads + loads:
        copy.start()

    barrier = pltpu.get_barrier_semaphore()

    def greet(seq, chan):
        pl.semaphore_signal(barrier, inc=1, device_id=(seq, chan), device_id_type=MESH)

    def greet_seq(d, _):
        greet(lax.rem(me + d, seq_size), mc)
        return 0

    lax.fori_loop(1, seq_size, greet_seq, 0)
    greet(me, mc + 1 - 2 * core)
    greet(pair_chip, near * 2 + core)
    for step in range(1, NODES):
        greet(me, lax.rem(node + step, NODES) * 2 + core)

    def exchange(src_of, dst, send_sem, recv_sem):
        pltpu.make_async_copy(src_of(me), dst, recv_sem).start()

        def send(d, _):
            peer = (
                lax.rem(px + d // 8, 4) * 8
                + lax.rem(py + lax.rem(d // 2, 4), 4) * 2
                + lax.rem(low + d, 2)
            )
            remote(src_of(peer), dst, send_sem, recv_sem, peer, mc).start()
            return 0

        lax.fori_loop(1, seq_size, send, 0)

    def pass_near():
        block = weight.at[node, mine]
        return remote(block, block, ws.at[0], wr.at[0], pair_chip, near * 2 + core)

    def pass_pair():
        block = weight.at[near, mine]
        return remote(block, block, ws.at[1], wr.at[1], pair_chip, mc)

    def pass_across():
        block = weight.at[far, mine, pl.ds(pl.multiple_of(low * 64, 64), 64)]
        return remote(block, block, ws.at[2], wr.at[2], pair_chip, near * 2 + core)

    def pass_across_pair():
        block = weight.at[across, mine, pl.ds(pl.multiple_of(64 - low * 64, 64), 64)]
        return remote(block, block, ws.at[3], wr.at[3], pair_chip, mc)

    def pass_beside(slot, which):
        for e, seq in enumerate(beside):
            block = weight.at[which, mine, pl.ds(e * 32, 32)]
            remote(block, block, es.at[slot], er.at[slot], seq, mc).start()

    for copy in mixed_loads:
        copy.wait()
    for pair in range(4):
        halves = []
        for a in (2 * pair, 2 * pair + 1):
            rows = slice(a * COLS, (a + 1) * COLS)
            mixed = (gate_in[rows, :].astype(F32) * value[rows, :].astype(F32)).astype(BF16)
            halves.append(mixed.astype(F32).T.reshape(seq_size, CH, LANE))
        xsend[:, pair * 16 : (pair + 1) * 16, :] = jnp.concatenate(halves, axis=1).astype(BF16)

    weight_load.wait()
    pl.semaphore_wait(barrier, seq_size - 1 + 5)
    pass_near().start()
    exchange(lambda peer: xsend.at[peer], xrecv.at[me], xs, xr)

    for part in range(2):
        spec_loads[part].wait()

        def turn_row(k, _):
            start = pl.multiple_of(k * width, width)
            hwide[pl.ds(start, width), :] = spec_buf[part, k].T
            return 0

        lax.fori_loop(0, BAND, turn_row, 0)

        def pack(dest, _):
            for c in range(CH):
                rows = hwide[pl.ds(dest * CH + c, BAND, stride=width), :]
                hsend[part, dest, c * BAND : (c + 1) * BAND, :] = rows.astype(BF16)
            return 0

        lax.fori_loop(0, seq_size, pack, 0)
        exchange(
            lambda peer: hsend.at[part, peer],
            hrecv.at[part, me],
            hs.at[part],
            hr.at[part, px],
        )

    for copy in loads:
        copy.wait()
    pltpu.make_async_copy(xsend, xrecv, xr).wait()
    pass_near().wait_recv()
    pass_pair().start()
    xwide[...] = xrecv[...].astype(F32).reshape(seq_size * 64, LANE)
    for c in range(CH):
        xgrid[:, c * LANE : (c + 1) * LANE] = xwide[pl.ds(c, half_rows, stride=CH), :].astype(BF16)

    def forward(g, _):
        rows = pl.ds(pl.multiple_of(g * krows, krows), krows)
        rows_im = pl.ds(pl.multiple_of(row_count + g * krows, krows), krows)
        cos, sin = turn[0, rows, :], turn[1, rows, :]
        for pair in range(CH // 2):
            x = xgrid[:, pair * 256 : (pair + 1) * 256]
            re = mm(fwd_row[0, rows, :], x) + mm(fwd_row[1, rows, :], x)
            im = mm(fwd_row[0, rows_im, :], x) + mm(fwd_row[1, rows_im, :], x)
            for h in range(2):
                r = re[:, h * LANE : (h + 1) * LANE]
                i = im[:, h * LANE : (h + 1) * LANE]
                turned = jnp.concatenate([r * cos + i * sin, i * cos - r * sin], axis=1)
                high = turned.astype(BF16)
                rest = (turned - high.astype(F32)).astype(BF16)
                freq[2 * pair + h, rows, :] = (
                    mm(high, fwd_col[0]) + mm(high, fwd_col[1]) + mm(rest, fwd_col[0])
                )
        return 0

    lax.fori_loop(0, groups, forward, 0)
    pass_pair().wait_recv()
    pass_across().start()
    pass_beside(0, near)
    pass_beside(1, far)

    total[...] = jnp.zeros_like(total)

    def inverse(step, _):
        g = lax.rem(px + groups - step, groups)
        members_at = pl.ds(pl.multiple_of(g * members, members), members)
        for part in range(2):
            block = hrecv.at[part, members_at]
            pltpu.make_async_copy(hsend.at[part, members_at], block, hr.at[part, g]).wait()
        rows = pl.ds(pl.multiple_of(g * krows, krows), krows)
        cos, sin = turn[0, rows, :], turn[1, rows, :]
        for c in range(CH):
            band = slice(c * BAND, (c + 1) * BAND)
            h_re = hrecv[0, members_at, band, :].astype(F32).reshape(krows, LANE)
            h_im = hrecv[1, members_at, band, :].astype(F32).reshape(krows, LANE)
            f_re, f_im = freq[c, rows, :LANE], freq[c, rows, LANE:]
            prod = jnp.concatenate([f_re * h_re - f_im * h_im, f_re * h_im + f_im * h_re], axis=1)
            prod = prod.astype(BF16)
            grid = mm(prod, inv_col[0]) + mm(prod, inv_col[1])
            b_re, b_im = grid[:, :LANE], grid[:, LANE:]
            lanes = slice(c * LANE, (c + 1) * LANE)
            back[:krows, lanes] = (b_re * cos - b_im * sin).astype(BF16)
            back[krows:, lanes] = (b_re * sin + b_im * cos).astype(BF16)
        for pair in range(CH // 2):
            lanes = slice(pair * 256, (pair + 1) * 256)
            total[:, lanes] += mm(inv_row[0, g], back[:, lanes]) + mm(inv_row[1, g], back[:, lanes])
        return 0

    lax.fori_loop(0, groups - 1, inverse, 0)
    pass_across().wait_recv()
    pass_across_pair().start()
    inverse(groups - 1, 0)

    for pair in range(CH // 2):
        halves = []
        for c in (2 * pair, 2 * pair + 1):
            lanes = slice(c * LANE, (c + 1) * LANE)
            inner = total[:, lanes] + skip[me * CH + c] * xgrid[:, lanes].astype(F32)
            halves.append(inner.reshape(seq_size, 8, LANE))
        ysend[:, pair * 16 : (pair + 1) * 16, :] = jnp.concatenate(halves, axis=1).astype(BF16)
    exchange(lambda peer: ysend.at[peer], yrecv.at[me], ys, yr)
    pass_across_pair().wait_recv()
    pass_beside(2, across)
    pltpu.make_async_copy(ysend, yrecv, yr).wait()
    ywide[...] = yrecv[...].astype(F32).reshape(seq_size * 64, LANE)

    for step in (2, 1, 3, 0):
        dest = lax.rem(node + step, NODES)
        for h in range(2):
            a = dest * 2 + h
            inner = ywide[pl.ds(a, width, stride=8), :].T
            gate = gate_out[pl.ds(pl.multiple_of(a * COLS, COLS), COLS), :]
            gsend[dest, h] = (gate.astype(F32) * inner).astype(BF16)
        if step:
            remote(
                gsend.at[dest], grecv.at[node], gs.at[step], gr.at[node], me, dest * 2 + core
            ).start()

    def product(rows_of, which, n):
        rows = rows_of.reshape(2 * COLS, width)
        lanes = slice(n * SPAN, (n + 1) * SPAN)
        return mm(rows, weight[which, :, :, lanes].reshape(width, SPAN)).reshape(2, COLS, SPAN)

    for n in range(SPANS):
        partial[n] = product(gsend[node], node, n)
    for slot, which in enumerate((near, far, across)):
        pltpu.make_async_copy(gsend.at[which], grecv.at[which], gr.at[which]).wait()
        half = weight.at[which, 1 - mine]
        pltpu.make_async_copy(half, half, er.at[slot]).wait()
        rows = grecv[which]
        for n in range(SPANS):
            partial[n] += product(rows, which, n)
            if slot == 2:
                remote(
                    partial.at[n, 1 - core],
                    mate_part.at[n],
                    ms.at[n],
                    mr.at[n],
                    me,
                    mc + 1 - 2 * core,
                ).start()
    for n in range(SPANS):
        pltpu.make_async_copy(mate_part.at[n], mate_part.at[n], mr.at[n]).wait()
        out[:, n * SPAN : (n + 1) * SPAN] = (partial[n, core] + mate_part[n]).astype(BF16)

    others = pl.ds(0, seq_size - 1)
    pltpu.make_async_copy(xsend.at[others], xrecv.at[others], xs).wait()
    for part in range(2):
        pltpu.make_async_copy(hsend.at[part, others], hrecv.at[part, others], hs.at[part]).wait()
    pltpu.make_async_copy(ysend.at[others], yrecv.at[others], ys).wait()
    for step in range(1, NODES):
        pltpu.make_async_copy(gsend.at[0], grecv.at[0], gs.at[step]).wait()
    for n in range(SPANS):
        pltpu.make_async_copy(mate_part.at[n], mate_part.at[n], ms.at[n]).wait()
    pass_near().wait_send()
    pass_pair().wait_send()
    pass_across().wait_send()
    pass_across_pair().wait_send()
    for slot in range(3):
        half = weight.at[0, 0]
        pltpu.make_async_copy(half, half, es.at[slot]).wait()


def local(value, gate_in, gate_out, skip_weight, spectrum, out_weight):
    seq_size = lax.axis_size("seq")
    half_rows = 8 * seq_size
    row_count = 2 * half_rows
    width = CH * seq_size
    features = out_weight.shape[1]
    groups = seq_size // GROUP
    krows = GROUP * BAND
    mats = constants(seq_size)
    vmem = pl.BlockSpec(memory_space=pltpu.VMEM)
    smem = pl.BlockSpec(memory_space=pltpu.SMEM)
    hbm = pl.BlockSpec(memory_space=pl.ANY)
    dma = pltpu.SemaphoreType.DMA
    return pl.pallas_call(
        functools.partial(conv_kernel, seq_size),
        out_shape=jax.ShapeDtypeStruct((COLS, features), BF16),
        in_specs=[hbm, hbm, hbm, smem, hbm, hbm] + [hbm] * 5,
        out_specs=vmem,
        scratch_shapes=[
            *[pltpu.VMEM(m.shape, F32 if m.dtype == np.float32 else BF16) for m in mats],
            pltpu.VMEM((1024, width), BF16),
            pltpu.VMEM((1024, width), BF16),
            pltpu.VMEM((1024, width), BF16),
            pltpu.VMEM((2, BAND, COLS, width), F32),
            pltpu.VMEM((NODES, 2, width // 2, features), BF16),
            pltpu.VMEM((seq_size, 64, LANE), BF16),
            pltpu.VMEM((seq_size, 64, LANE), BF16),
            pltpu.VMEM((seq_size * 64, LANE), F32),
            pltpu.VMEM((half_rows, CH * LANE), BF16),
            pltpu.VMEM((BAND * width, LANE), F32),
            pltpu.VMEM((2, seq_size, CH * BAND, LANE), BF16),
            pltpu.VMEM((2, seq_size, CH * BAND, LANE), BF16),
            pltpu.VMEM((CH, row_count, 2 * LANE), F32),
            pltpu.VMEM((2 * krows, CH * LANE), BF16),
            pltpu.VMEM((half_rows, CH * LANE), F32),
            pltpu.VMEM((seq_size, 64, LANE), BF16),
            pltpu.VMEM((seq_size, 64, LANE), BF16),
            pltpu.VMEM((seq_size * 64, LANE), F32),
            pltpu.VMEM((NODES, 2, COLS, width), BF16),
            pltpu.VMEM((NODES, 2, COLS, width), BF16),
            pltpu.VMEM((SPANS, 2, COLS, SPAN), F32),
            pltpu.VMEM((SPANS, COLS, SPAN), F32),
            dma((9,)),
            dma((2,)),
            dma,
            dma,
            dma((2,)),
            dma((2, groups)),
            dma,
            dma,
            dma((NODES,)),
            dma((NODES,)),
            dma((4,)),
            dma((4,)),
            dma((3,)),
            dma((3,)),
            dma((SPANS,)),
            dma((SPANS,)),
        ],
        compiler_params=pltpu.CompilerParams(
            collective_id=0, has_side_effects=True, vmem_limit_bytes=60 * 1024 * 1024
        ),
        name="long_conv",
    )(
        value,
        gate_in,
        gate_out,
        skip_weight,
        spectrum,
        out_weight.reshape(2, width // 2, features),
        *[jnp.asarray(m) for m in mats],
    )


def solution(mesh):
    placed = (
        P("seq", "chan"),
        P("seq", "chan"),
        P("seq", "chan"),
        P("chan"),
        P(None, "seq", None, "chan"),
        P("chan", None),
    )
    return jax.shard_map(
        local, mesh=mesh, in_specs=placed, out_specs=P(("seq", "chan"), None), check_vma=False
    )
```

```python
import functools
import math

import jax
import jax.numpy as jnp
import ml_dtypes
import numpy as np
from jax import lax
from jax.experimental import pallas as pl
from jax.experimental.pallas import tpu as pltpu
from jax.sharding import PartitionSpec as P

COLS = 128
LANE = 128
CH = 8
BAND = 16
GROUP = 8
NODES = 4
QUARTERS = 4
SPANS, SPAN = 4, 512
MESH = pl.DeviceIdType.MESH
F32 = jnp.float32
BF16 = jnp.bfloat16


def two_terms(matrix):
    high = matrix.astype(np.float32).astype(ml_dtypes.bfloat16)
    low = (matrix - high.astype(np.float64)).astype(np.float32).astype(ml_dtypes.bfloat16)
    return np.stack([high, low])


def constants(seq_size):
    half_rows = 8 * seq_size
    row_count = 2 * half_rows
    padded_len = row_count * COLS
    k1 = np.arange(row_count)
    a = np.arange(half_rows)
    b = np.arange(COLS)
    row = 2.0 * np.pi / row_count * (np.outer(k1, a) % row_count)
    fwd_row = np.concatenate([np.cos(row), -np.sin(row)], axis=0)
    twist = 2.0 * np.pi / padded_len * (np.outer(k1, b) % padded_len)
    turn = np.stack([np.cos(twist), np.sin(twist)]).astype(np.float32)
    col = 2.0 * np.pi / COLS * (np.outer(b, b) % COLS)
    cos, sin = np.cos(col), np.sin(col)
    fwd_col = np.block([[cos, -sin], [sin, cos]])
    inv_col = np.block([[cos, sin], [-sin, cos]])
    groups = seq_size // min(GROUP, seq_size)
    back = row.T.reshape(half_rows, groups, -1)
    inv_row = np.concatenate([np.cos(back), -np.sin(back)], axis=2) / padded_len
    inv_row = np.ascontiguousarray(inv_row.transpose(1, 0, 2))
    return two_terms(fwd_row), turn, two_terms(fwd_col), two_terms(inv_col), two_terms(inv_row)


def mm(x, y):
    return jnp.dot(x, y, preferred_element_type=F32)


def conv_kernel(
    seq_size,
    value_hbm,
    gate_in_hbm,
    gate_out_hbm,
    skip,
    spectrum,
    weight_hbm,
    fwd_row_hbm,
    turn_hbm,
    fwd_col_hbm,
    inv_col_hbm,
    inv_row_hbm,
    out,
    fwd_row,
    turn,
    fwd_col,
    inv_col,
    inv_row,
    value,
    gate_in,
    gate_out,
    spec_buf,
    weight,
    xsend,
    xrecv,
    xwide,
    xgrid,
    hwide,
    hsend,
    hrecv,
    freq,
    back,
    total,
    ysend,
    yrecv,
    ywide,
    gsend,
    grecv,
    partial,
    mate_part,
    load_sem,
    spec_sem,
    xs,
    xr,
    hs,
    hr,
    ys,
    yr,
    gs,
    gr,
    ws,
    wr,
    es,
    er,
    ms,
    mr,
):
    me = lax.axis_index("seq")
    mc = lax.axis_index("chan")
    half_rows = 8 * seq_size
    row_count = 2 * half_rows
    width = CH * seq_size
    members = GROUP
    groups = seq_size // members
    krows = members * BAND
    px, py, low = me // 8, lax.rem(me // 2, 4), lax.rem(me, 2)
    node, core = mc // 2, lax.rem(mc, 2)
    pair_chip = me + 1 - 2 * low
    near = lax.rem(node + 3 + 2 * low, NODES)
    far = lax.rem(node + 5 - 2 * low, NODES)
    across = lax.rem(node + 2, NODES)
    mine = lax.rem(px + 2 * py, QUARTERS)
    beside = [
        lax.rem(px + 1, 4) * 8 + py * 2 + low,
        lax.rem(px + 3, 4) * 8 + py * 2 + low,
        px * 8 + lax.rem(py + 1, 4) * 2 + low,
        px * 8 + lax.rem(py + 3, 4) * 2 + low,
    ]

    def remote(src, dst, send_sem, recv_sem, seq, chan):
        return pltpu.make_async_remote_copy(
            src_ref=src,
            dst_ref=dst,
            send_sem=send_sem,
            recv_sem=recv_sem,
            device_id=(seq, chan),
            device_id_type=MESH,
        )

    mixed_loads = [
        pltpu.make_async_copy(value_hbm, value, load_sem.at[6]),
        pltpu.make_async_copy(gate_in_hbm, gate_in, load_sem.at[7]),
    ]
    weight_load = pltpu.make_async_copy(weight_hbm, weight.at[node], load_sem.at[8])
    loads = [
        pltpu.make_async_copy(fwd_row_hbm, fwd_row, load_sem.at[0]),
        pltpu.make_async_copy(turn_hbm, turn, load_sem.at[1]),
        pltpu.make_async_copy(fwd_col_hbm, fwd_col, load_sem.at[2]),
        pltpu.make_async_copy(inv_col_hbm, inv_col, load_sem.at[3]),
        pltpu.make_async_copy(inv_row_hbm, inv_row, load_sem.at[4]),
        pltpu.make_async_copy(gate_out_hbm, gate_out, load_sem.at[5]),
    ]
    spec_loads = [
        pltpu.make_async_copy(spectrum.at[part], spec_buf.at[part], spec_sem.at[part])
        for part in range(2)
    ]
    for copy in mixed_loads + [weight_load] + spec_loads + loads:
        copy.start()

    barrier = pltpu.get_barrier_semaphore()

    def greet(seq, chan):
        pl.semaphore_signal(barrier, inc=1, device_id=(seq, chan), device_id_type=MESH)

    def greet_seq(d, _):
        greet(lax.rem(me + d, seq_size), mc)
        return 0

    lax.fori_loop(1, seq_size, greet_seq, 0)
    greet(me, mc + 1 - 2 * core)
    greet(pair_chip, near * 2 + core)
    for step in range(1, NODES):
        greet(me, lax.rem(node + step, NODES) * 2 + core)

    def exchange(src_of, dst, send_sem, recv_sem):
        pltpu.make_async_copy(src_of(me), dst, recv_sem).start()

        def send(d, _):
            peer = (
                lax.rem(px + d // 8, 4) * 8
                + lax.rem(py + lax.rem(d // 2, 4), 4) * 2
                + lax.rem(low + d, 2)
            )
            remote(src_of(peer), dst, send_sem, recv_sem, peer, mc).start()
            return 0

        lax.fori_loop(1, seq_size, send, 0)

    def pass_near(step):
        block = weight.at[node, lax.rem(mine + step, QUARTERS)]
        sem = min(step, 1)
        return remote(block, block, ws.at[sem], wr.at[sem], pair_chip, near * 2 + core)

    def pass_pair():
        block = weight.at[near, mine]
        return remote(block, block, ws.at[2], wr.at[2], pair_chip, mc)

    def pass_across():
        block = weight.at[far, mine, pl.ds(pl.multiple_of(low * 32, 32), 32)]
        return remote(block, block, ws.at[3], wr.at[3], pair_chip, near * 2 + core)

    def pass_across_pair():
        block = weight.at[across, mine, pl.ds(pl.multiple_of(32 - low * 32, 32), 32)]
        return remote(block, block, ws.at[4], wr.at[4], pair_chip, mc)

    def pass_beside(slot, which):
        for e, seq in enumerate(beside):
            rows = pl.ds(0, 64) if e < 2 else pl.ds((e - 2) * 32, 32)
            block = weight.at[which, mine, rows]
            remote(block, block, es.at[slot], er.at[slot], seq, mc).start()

    def channel(dest, c):
        return (c // 4) * (width // 2) + dest * 4 + c % 4

    for copy in mixed_loads:
        copy.wait()
    for a in range(8):
        rows = slice(a * COLS, (a + 1) * COLS)
        mixed = (gate_in[rows, :].astype(F32) * value[rows, :].astype(F32)).astype(BF16)
        xwide[a * width : (a + 1) * width, :] = mixed.astype(F32).T

    def pack_input(dest, _):
        for pair in range(CH // 2):
            rows = [
                xwide[pl.ds(channel(dest, c), 8, stride=width), :] for c in (2 * pair, 2 * pair + 1)
            ]
            xsend[dest, pair * 16 : (pair + 1) * 16, :] = jnp.concatenate(rows).astype(BF16)
        return 0

    lax.fori_loop(0, seq_size, pack_input, 0)

    weight_load.wait()
    pl.semaphore_wait(barrier, seq_size - 1 + 5)
    pass_near(0).start()
    exchange(lambda peer: xsend.at[peer], xrecv.at[me], xs, xr)
    for step in range(1, QUARTERS):
        pass_near(step).start()

    for part in range(2):
        spec_loads[part].wait()

        def turn_row(k, _):
            start = pl.multiple_of(k * width, width)
            hwide[pl.ds(start, width), :] = spec_buf[part, k].T
            return 0

        lax.fori_loop(0, BAND, turn_row, 0)

        def pack(dest, _):
            for c in range(CH):
                rows = hwide[pl.ds(channel(dest, c), BAND, stride=width), :]
                hsend[part, dest, c * BAND : (c + 1) * BAND, :] = rows.astype(BF16)
            return 0

        lax.fori_loop(0, seq_size, pack, 0)
        exchange(
            lambda peer: hsend.at[part, peer],
            hrecv.at[part, me],
            hs.at[part],
            hr.at[part, px],
        )
        if part == 0:
            pass_near(0).wait_recv()
            pass_pair().start()

    for copy in loads:
        copy.wait()
    pltpu.make_async_copy(xsend, xrecv, xr).wait()
    for c in range(CH):
        pair = xrecv[:, c // 2 * 16 : c // 2 * 16 + 16, :].astype(F32)
        rows = pair[:, c % 2 * 8 : c % 2 * 8 + 8, :].reshape(half_rows, LANE)
        xgrid[:, c * LANE : (c + 1) * LANE] = rows.astype(BF16)
    pass_pair().wait_recv()
    pass_across().start()
    pass_beside(0, far)

    def forward(g, _):
        rows = pl.ds(pl.multiple_of(g * krows, krows), krows)
        rows_im = pl.ds(pl.multiple_of(row_count + g * krows, krows), krows)
        cos, sin = turn[0, rows, :], turn[1, rows, :]
        for pair in range(CH // 2):
            x = xgrid[:, pair * 256 : (pair + 1) * 256]
            re = mm(fwd_row[0, rows, :], x) + mm(fwd_row[1, rows, :], x)
            im = mm(fwd_row[0, rows_im, :], x) + mm(fwd_row[1, rows_im, :], x)
            for h in range(2):
                r = re[:, h * LANE : (h + 1) * LANE]
                i = im[:, h * LANE : (h + 1) * LANE]
                turned = jnp.concatenate([r * cos + i * sin, i * cos - r * sin], axis=1)
                high = turned.astype(BF16)
                rest = (turned - high.astype(F32)).astype(BF16)
                freq[2 * pair + h, rows, :] = (
                    mm(high, fwd_col[0]) + mm(high, fwd_col[1]) + mm(rest, fwd_col[0])
                )
        return 0

    lax.fori_loop(0, groups, forward, 0)
    pass_across().wait_recv()
    pass_across_pair().start()

    total[...] = jnp.zeros_like(total)

    def inverse(step, channels):
        g = lax.rem(px + groups - step, groups)
        members_at = pl.ds(pl.multiple_of(g * members, members), members)
        if 0 in channels:
            for part in range(2):
                block = hrecv.at[part, members_at]
                pltpu.make_async_copy(hsend.at[part, members_at], block, hr.at[part, g]).wait()
        rows = pl.ds(pl.multiple_of(g * krows, krows), krows)
        cos, sin = turn[0, rows, :], turn[1, rows, :]
        for c in channels:
            band = slice(c * BAND, (c + 1) * BAND)
            h_re = hrecv[0, members_at, band, :].astype(F32).reshape(krows, LANE)
            h_im = hrecv[1, members_at, band, :].astype(F32).reshape(krows, LANE)
            f_re, f_im = freq[c, rows, :LANE], freq[c, rows, LANE:]
            prod = jnp.concatenate([f_re * h_re - f_im * h_im, f_re * h_im + f_im * h_re], axis=1)
            prod = prod.astype(BF16)
            grid = mm(prod, inv_col[0]) + mm(prod, inv_col[1])
            b_re, b_im = grid[:, :LANE], grid[:, LANE:]
            lanes = slice(c * LANE, (c + 1) * LANE)
            back[:krows, lanes] = (b_re * cos - b_im * sin).astype(BF16)
            back[krows:, lanes] = (b_re * sin + b_im * cos).astype(BF16)
        for pair in range(channels[0] // 2, channels[-1] // 2 + 1):
            lanes = slice(pair * 256, (pair + 1) * 256)
            total[:, lanes] += mm(inv_row[0, g], back[:, lanes]) + mm(inv_row[1, g], back[:, lanes])

    def inverse_all(step, _):
        inverse(step, range(CH))
        return 0

    lax.fori_loop(0, groups - 1, inverse_all, 0)

    for part in range(2):
        inverse(groups - 1, range(part * 4, part * 4 + 4))
        for pair in range(2):
            halves = []
            for c in (part * 4 + 2 * pair, part * 4 + 2 * pair + 1):
                lanes = slice(c * LANE, (c + 1) * LANE)
                direct = skip[channel(me, c)] * xgrid[:, lanes].astype(F32)
                halves.append((total[:, lanes] + direct).reshape(seq_size, 8, LANE))
            rows = slice(pair * 16, (pair + 1) * 16)
            ysend[part, :, rows, :] = jnp.concatenate(halves, axis=1).astype(BF16)
        exchange(
            lambda peer: ysend.at[part, peer], yrecv.at[part, me], ys.at[part], yr.at[part]
        )

    for part in range(2):
        pltpu.make_async_copy(ysend.at[part], yrecv.at[part], yr.at[part]).wait()
        ywide[...] = yrecv[part].astype(F32).reshape(seq_size * 32, LANE)
        for step in (2, 1, 3, 0):
            dest = lax.rem(node + step, NODES)
            for h in range(2):
                a = dest * 2 + h
                inner = ywide[pl.ds(a, width // 2, stride=8), :].T
                gate = gate_out[
                    pl.ds(pl.multiple_of(a * COLS, COLS), COLS), part * LANE : (part + 1) * LANE
                ]
                gsend[part, dest, h] = (gate.astype(F32) * inner).astype(BF16)
            if step:
                remote(
                    gsend.at[part, dest],
                    grecv.at[part, node],
                    gs.at[part, step],
                    gr.at[part, node],
                    me,
                    dest * 2 + core,
                ).start()
    pass_across_pair().wait_recv()
    pass_beside(1, across)

    def product(sources, n):
        lanes = slice(n * SPAN, (n + 1) * SPAN)
        rows = jnp.concatenate([r.reshape(2 * COLS, LANE) for r, _, _ in sources], axis=1)
        block = jnp.concatenate(
            [weight[w, 2 * p : 2 * p + 2, :, lanes].reshape(LANE, SPAN) for _, w, p in sources]
        )
        return mm(rows, block).reshape(2, COLS, SPAN)

    def arrive(part, which):
        pltpu.make_async_copy(
            gsend.at[part, which], grecv.at[part, which], gr.at[part, which]
        ).wait()

    for n in range(SPANS):
        partial[n] = product([(gsend[p, node], node, p) for p in range(2)], n)
    rest = weight.at[near, pl.ds(0, QUARTERS - 1)]
    pltpu.make_async_copy(rest, rest, wr.at[1]).wait()
    pltpu.make_async_copy(rest, rest, er.at[0]).wait()
    for part in range(2):
        arrive(part, near)
        arrive(part, far)
        for n in range(SPANS):
            partial[n] += product([(grecv[part, w], w, part) for w in (near, far)], n)
    pltpu.make_async_copy(rest, rest, er.at[1]).wait()
    for part in range(2):
        arrive(part, across)
    for n in range(SPANS):
        partial[n] += product([(grecv[p, across], across, p) for p in range(2)], n)
        remote(
            partial.at[n, 1 - core],
            mate_part.at[n],
            ms.at[n],
            mr.at[n],
            me,
            mc + 1 - 2 * core,
        ).start()
    for n in range(SPANS):
        pltpu.make_async_copy(mate_part.at[n], mate_part.at[n], mr.at[n]).wait()
        out[:, n * SPAN : (n + 1) * SPAN] = (partial[n, core] + mate_part[n]).astype(BF16)

    others = pl.ds(0, seq_size - 1)
    pltpu.make_async_copy(xsend.at[others], xrecv.at[others], xs).wait()
    for part in range(2):
        pltpu.make_async_copy(hsend.at[part, others], hrecv.at[part, others], hs.at[part]).wait()
    for part in range(2):
        pltpu.make_async_copy(ysend.at[part, others], yrecv.at[part, others], ys.at[part]).wait()
        for step in range(1, NODES):
            pltpu.make_async_copy(gsend.at[0, 0], grecv.at[0, 0], gs.at[part, step]).wait()
    for n in range(SPANS):
        pltpu.make_async_copy(mate_part.at[n], mate_part.at[n], ms.at[n]).wait()
    pass_near(0).wait_send()
    pltpu.make_async_copy(rest, rest, ws.at[1]).wait()
    pass_pair().wait_send()
    pass_across().wait_send()
    pass_across_pair().wait_send()
    for slot in range(2):
        pltpu.make_async_copy(rest, rest, es.at[slot]).wait()


def local(value, gate_in, gate_out, skip_weight, spectrum, out_weight):
    seq_size = lax.axis_size("seq")
    half_rows = 8 * seq_size
    row_count = 2 * half_rows
    width = CH * seq_size
    features = out_weight.shape[1]
    groups = seq_size // GROUP
    krows = GROUP * BAND
    mats = constants(seq_size)
    vmem = pl.BlockSpec(memory_space=pltpu.VMEM)
    smem = pl.BlockSpec(memory_space=pltpu.SMEM)
    hbm = pl.BlockSpec(memory_space=pl.ANY)
    dma = pltpu.SemaphoreType.DMA
    return pl.pallas_call(
        functools.partial(conv_kernel, seq_size),
        out_shape=jax.ShapeDtypeStruct((COLS, features), BF16),
        in_specs=[hbm, hbm, hbm, smem, hbm, hbm] + [hbm] * 5,
        out_specs=vmem,
        scratch_shapes=[
            *[pltpu.VMEM(m.shape, F32 if m.dtype == np.float32 else BF16) for m in mats],
            pltpu.VMEM((1024, width), BF16),
            pltpu.VMEM((1024, width), BF16),
            pltpu.VMEM((1024, width), BF16),
            pltpu.VMEM((2, BAND, COLS, width), F32),
            pltpu.VMEM((NODES, QUARTERS, width // QUARTERS, features), BF16),
            pltpu.VMEM((seq_size, 64, LANE), BF16),
            pltpu.VMEM((seq_size, 64, LANE), BF16),
            pltpu.VMEM((seq_size * 64, LANE), F32),
            pltpu.VMEM((half_rows, CH * LANE), BF16),
            pltpu.VMEM((BAND * width, LANE), F32),
            pltpu.VMEM((2, seq_size, CH * BAND, LANE), BF16),
            pltpu.VMEM((2, seq_size, CH * BAND, LANE), BF16),
            pltpu.VMEM((CH, row_count, 2 * LANE), F32),
            pltpu.VMEM((2 * krows, CH * LANE), BF16),
            pltpu.VMEM((half_rows, CH * LANE), F32),
            pltpu.VMEM((2, seq_size, 32, LANE), BF16),
            pltpu.VMEM((2, seq_size, 32, LANE), BF16),
            pltpu.VMEM((seq_size * 32, LANE), F32),
            pltpu.VMEM((2, NODES, 2, COLS, LANE), BF16),
            pltpu.VMEM((2, NODES, 2, COLS, LANE), BF16),
            pltpu.VMEM((SPANS, 2, COLS, SPAN), F32),
            pltpu.VMEM((SPANS, COLS, SPAN), F32),
            dma((9,)),
            dma((2,)),
            dma,
            dma,
            dma((2,)),
            dma((2, groups)),
            dma((2,)),
            dma((2,)),
            dma((2, NODES)),
            dma((2, NODES)),
            dma((5,)),
            dma((5,)),
            dma((2,)),
            dma((2,)),
            dma((SPANS,)),
            dma((SPANS,)),
        ],
        compiler_params=pltpu.CompilerParams(
            collective_id=0, has_side_effects=True, vmem_limit_bytes=60 * 1024 * 1024
        ),
        name="long_conv",
    )(
        value,
        gate_in,
        gate_out,
        skip_weight,
        spectrum,
        out_weight.reshape(QUARTERS, width // QUARTERS, features),
        *[jnp.asarray(m) for m in mats],
    )


def solution(mesh):
    placed = (
        P("seq", "chan"),
        P("seq", "chan"),
        P("seq", "chan"),
        P("chan"),
        P(None, "seq", None, "chan"),
        P("chan", None),
    )
    return jax.shard_map(
        local, mesh=mesh, in_specs=placed, out_specs=P(("seq", "chan"), None), check_vma=False
    )
```

```python
import functools
import math

import jax
import jax.numpy as jnp
import ml_dtypes
import numpy as np
from jax import lax
from jax.experimental import pallas as pl
from jax.experimental.pallas import tpu as pltpu
from jax.sharding import PartitionSpec as P

COLS = 128
LANE = 128
CH = 8
BAND = 16
GROUP = 8
NODES = 4
QUARTERS = 4
SPANS, SPAN = 4, 512
MESH = pl.DeviceIdType.MESH
F32 = jnp.float32
BF16 = jnp.bfloat16


def two_terms(matrix):
    high = matrix.astype(np.float32).astype(ml_dtypes.bfloat16)
    low = (matrix - high.astype(np.float64)).astype(np.float32).astype(ml_dtypes.bfloat16)
    return np.stack([high, low])


def constants(seq_size):
    half_rows = 8 * seq_size
    row_count = 2 * half_rows
    padded_len = row_count * COLS
    k1 = np.arange(row_count)
    a = np.arange(half_rows)
    b = np.arange(COLS)
    row = 2.0 * np.pi / row_count * (np.outer(k1, a) % row_count)
    fwd_row = np.concatenate([np.cos(row), -np.sin(row)], axis=0)
    twist = 2.0 * np.pi / padded_len * (np.outer(k1, b) % padded_len)
    turn = np.stack([np.cos(twist), np.sin(twist)]).astype(np.float32)
    col = 2.0 * np.pi / COLS * (np.outer(b, b) % COLS)
    cos, sin = np.cos(col), np.sin(col)
    fwd_col = np.block([[cos, -sin], [sin, cos]])
    inv_col = np.block([[cos, sin], [-sin, cos]])
    groups = seq_size // min(GROUP, seq_size)
    back = row.T.reshape(half_rows, groups, -1)
    inv_row = np.concatenate([np.cos(back), -np.sin(back)], axis=2) / padded_len
    inv_row = np.ascontiguousarray(inv_row.transpose(1, 0, 2))
    return two_terms(fwd_row), turn, two_terms(fwd_col), two_terms(inv_col), two_terms(inv_row)


def mm(x, y):
    return jnp.dot(x, y, preferred_element_type=F32)


def conv_kernel(
    seq_size,
    value_hbm,
    gate_in_hbm,
    gate_out_hbm,
    skip,
    spectrum,
    weight_hbm,
    fwd_row_hbm,
    turn_hbm,
    fwd_col_hbm,
    inv_col_hbm,
    inv_row_hbm,
    out,
    fwd_row,
    turn,
    fwd_col,
    inv_col,
    inv_row,
    value,
    gate_in,
    gate_out,
    spec_buf,
    weight,
    xsend,
    xrecv,
    xwide,
    xgrid,
    hwide,
    hsend,
    hrecv,
    freq,
    back,
    total,
    ysend,
    yrecv,
    ywide,
    gsend,
    grecv,
    partial,
    load_sem,
    spec_sem,
    xs,
    xr,
    hs,
    hr,
    ys,
    yr,
    gs,
    gr,
    ws,
    wr,
    es,
    er,
    cs,
    cr,
):
    me = lax.axis_index("seq")
    mc = lax.axis_index("chan")
    half_rows = 8 * seq_size
    row_count = 2 * half_rows
    width = CH * seq_size
    members = GROUP
    groups = seq_size // members
    krows = members * BAND
    px, py, low = me // 8, lax.rem(me // 2, 4), lax.rem(me, 2)
    node, core = mc // 2, lax.rem(mc, 2)
    pair_chip = me + 1 - 2 * low
    near = lax.rem(node + 3 + 2 * low, NODES)
    far = lax.rem(node + 5 - 2 * low, NODES)
    across = lax.rem(node + 2, NODES)
    mine = lax.rem(px + 2 * py, QUARTERS)
    beside = [
        lax.rem(px + 1, 4) * 8 + py * 2 + low,
        lax.rem(px + 3, 4) * 8 + py * 2 + low,
        px * 8 + lax.rem(py + 1, 4) * 2 + low,
        px * 8 + lax.rem(py + 3, 4) * 2 + low,
    ]

    def remote(src, dst, send_sem, recv_sem, seq, chan):
        return pltpu.make_async_remote_copy(
            src_ref=src,
            dst_ref=dst,
            send_sem=send_sem,
            recv_sem=recv_sem,
            device_id=(seq, chan),
            device_id_type=MESH,
        )

    mixed_loads = [
        pltpu.make_async_copy(value_hbm, value, load_sem.at[6]),
        pltpu.make_async_copy(gate_in_hbm, gate_in, load_sem.at[7]),
    ]
    weight_load = pltpu.make_async_copy(weight_hbm, weight.at[core, node], load_sem.at[8])
    loads = [
        pltpu.make_async_copy(fwd_row_hbm, fwd_row, load_sem.at[0]),
        pltpu.make_async_copy(turn_hbm, turn, load_sem.at[1]),
        pltpu.make_async_copy(fwd_col_hbm, fwd_col, load_sem.at[2]),
        pltpu.make_async_copy(inv_col_hbm, inv_col, load_sem.at[3]),
        pltpu.make_async_copy(inv_row_hbm, inv_row, load_sem.at[4]),
        pltpu.make_async_copy(gate_out_hbm, gate_out, load_sem.at[5]),
    ]
    spec_loads = [
        pltpu.make_async_copy(spectrum.at[part], spec_buf.at[part], spec_sem.at[part])
        for part in range(2)
    ]
    for copy in mixed_loads + [weight_load] + spec_loads + loads:
        copy.start()

    barrier = pltpu.get_barrier_semaphore()

    def greet(seq, chan):
        pl.semaphore_signal(barrier, inc=1, device_id=(seq, chan), device_id_type=MESH)

    def greet_seq(d, _):
        greet(lax.rem(me + d, seq_size), mc)
        return 0

    lax.fori_loop(1, seq_size, greet_seq, 0)
    greet(pair_chip, near * 2 + core)
    for step in range(1, 2 * NODES):
        greet(me, lax.rem(mc + step, 2 * NODES))

    def exchange(src_of, dst, send_sem, recv_sem):
        pltpu.make_async_copy(src_of(me), dst, recv_sem).start()

        def send(d, _):
            peer = (
                lax.rem(px + d // 8, 4) * 8
                + lax.rem(py + lax.rem(d // 2, 4), 4) * 2
                + lax.rem(low + d, 2)
            )
            remote(src_of(peer), dst, send_sem, recv_sem, peer, mc).start()
            return 0

        lax.fori_loop(1, seq_size, send, 0)

    def pass_near(step):
        block = weight.at[core, node, lax.rem(mine + step, QUARTERS)]
        sem = min(step, 1)
        return remote(block, block, ws.at[sem], wr.at[sem], pair_chip, near * 2 + core)

    def pass_pair():
        block = weight.at[core, near, mine]
        return remote(block, block, ws.at[2], wr.at[2], pair_chip, mc)

    def pass_across():
        block = weight.at[core, far, mine]
        return remote(block, block, ws.at[3], wr.at[3], pair_chip, near * 2 + core)

    def pass_beside(slot, which):
        for e, seq in enumerate(beside):
            rows = pl.ds(0, 64) if e < 2 else pl.ds((e - 2) * 32, 32)
            block = weight.at[core, which, mine, rows]
            remote(block, block, es.at[slot], er.at[slot], seq, mc).start()

    def hand_over(slot, which):
        block = weight.at[core, which]
        return remote(block, block, cs.at[slot], cr.at[slot], me, mc + 1 - 2 * core)

    def channel(dest, c):
        return (c // 4) * (width // 2) + dest * 4 + c % 4

    for copy in mixed_loads:
        copy.wait()
    for a in range(8):
        rows = slice(a * COLS, (a + 1) * COLS)
        mixed = (gate_in[rows, :].astype(F32) * value[rows, :].astype(F32)).astype(BF16)
        xwide[a * width : (a + 1) * width, :] = mixed.astype(F32).T

    def pack_input(dest, _):
        for pair in range(CH // 2):
            rows = [
                xwide[pl.ds(channel(dest, c), 8, stride=width), :] for c in (2 * pair, 2 * pair + 1)
            ]
            xsend[dest, pair * 16 : (pair + 1) * 16, :] = jnp.concatenate(rows).astype(BF16)
        return 0

    lax.fori_loop(0, seq_size, pack_input, 0)

    weight_load.wait()
    pl.semaphore_wait(barrier, seq_size - 1 + 2 * NODES)
    pass_near(0).start()
    exchange(lambda peer: xsend.at[peer], xrecv.at[me], xs, xr)
    for step in range(1, QUARTERS):
        pass_near(step).start()
    hand_over(0, node).start()

    for part in range(2):
        spec_loads[part].wait()

        def turn_row(k, _):
            start = pl.multiple_of(k * width, width)
            hwide[pl.ds(start, width), :] = spec_buf[part, k].T
            return 0

        lax.fori_loop(0, BAND, turn_row, 0)

        def pack(dest, _):
            for c in range(CH):
                rows = hwide[pl.ds(channel(dest, c), BAND, stride=width), :]
                hsend[part, dest, c * BAND : (c + 1) * BAND, :] = rows.astype(BF16)
            return 0

        lax.fori_loop(0, seq_size, pack, 0)
        exchange(
            lambda peer: hsend.at[part, peer],
            hrecv.at[part, me],
            hs.at[part],
            hr.at[part, px],
        )
        if part == 0:
            pass_near(0).wait_recv()
            pass_pair().start()

    for copy in loads:
        copy.wait()
    pltpu.make_async_copy(xsend, xrecv, xr).wait()
    for c in range(CH):
        pair = xrecv[:, c // 2 * 16 : c // 2 * 16 + 16, :].astype(F32)
        rows = pair[:, c % 2 * 8 : c % 2 * 8 + 8, :].reshape(half_rows, LANE)
        xgrid[:, c * LANE : (c + 1) * LANE] = rows.astype(BF16)
    pass_pair().wait_recv()
    pass_across().start()
    pass_beside(0, far)

    def forward(g, _):
        rows = pl.ds(pl.multiple_of(g * krows, krows), krows)
        rows_im = pl.ds(pl.multiple_of(row_count + g * krows, krows), krows)
        cos, sin = turn[0, rows, :], turn[1, rows, :]
        for pair in range(CH // 2):
            x = xgrid[:, pair * 256 : (pair + 1) * 256]
            re = mm(fwd_row[0, rows, :], x) + mm(fwd_row[1, rows, :], x)
            im = mm(fwd_row[0, rows_im, :], x) + mm(fwd_row[1, rows_im, :], x)
            for h in range(2):
                r = re[:, h * LANE : (h + 1) * LANE]
                i = im[:, h * LANE : (h + 1) * LANE]
                turned = jnp.concatenate([r * cos + i * sin, i * cos - r * sin], axis=1)
                high = turned.astype(BF16)
                rest = (turned - high.astype(F32)).astype(BF16)
                freq[2 * pair + h, rows, :] = (
                    mm(high, fwd_col[0]) + mm(high, fwd_col[1]) + mm(rest, fwd_col[0])
                )
        return 0

    lax.fori_loop(0, groups, forward, 0)
    total[...] = jnp.zeros_like(total)

    def inverse(step, channels):
        g = lax.rem(px + groups - step, groups)
        members_at = pl.ds(pl.multiple_of(g * members, members), members)
        if 0 in channels:
            for part in range(2):
                block = hrecv.at[part, members_at]
                pltpu.make_async_copy(hsend.at[part, members_at], block, hr.at[part, g]).wait()
        rows = pl.ds(pl.multiple_of(g * krows, krows), krows)
        cos, sin = turn[0, rows, :], turn[1, rows, :]
        for c in channels:
            band = slice(c * BAND, (c + 1) * BAND)
            h_re = hrecv[0, members_at, band, :].astype(F32).reshape(krows, LANE)
            h_im = hrecv[1, members_at, band, :].astype(F32).reshape(krows, LANE)
            f_re, f_im = freq[c, rows, :LANE], freq[c, rows, LANE:]
            prod = jnp.concatenate([f_re * h_re - f_im * h_im, f_re * h_im + f_im * h_re], axis=1)
            prod = prod.astype(BF16)
            grid = mm(prod, inv_col[0]) + mm(prod, inv_col[1])
            b_re, b_im = grid[:, :LANE], grid[:, LANE:]
            lanes = slice(c * LANE, (c + 1) * LANE)
            back[:krows, lanes] = (b_re * cos - b_im * sin).astype(BF16)
            back[krows:, lanes] = (b_re * sin + b_im * cos).astype(BF16)
        for pair in range(channels[0] // 2, channels[-1] // 2 + 1):
            lanes = slice(pair * 256, (pair + 1) * 256)
            total[:, lanes] += mm(inv_row[0, g], back[:, lanes]) + mm(inv_row[1, g], back[:, lanes])

    def inverse_all(step, _):
        inverse(step, range(CH))
        return 0

    lax.fori_loop(0, groups - 1, inverse_all, 0)

    for part in range(2):
        inverse(groups - 1, range(part * 4, part * 4 + 4))
        for pair in range(2):
            halves = []
            for c in (part * 4 + 2 * pair, part * 4 + 2 * pair + 1):
                lanes = slice(c * LANE, (c + 1) * LANE)
                direct = skip[channel(me, c)] * xgrid[:, lanes].astype(F32)
                halves.append((total[:, lanes] + direct).reshape(seq_size, 8, LANE))
            rows = slice(pair * 16, (pair + 1) * 16)
            ysend[part, :, rows, :] = jnp.concatenate(halves, axis=1).astype(BF16)
        exchange(
            lambda peer: ysend.at[part, peer], yrecv.at[part, me], ys.at[part], yr.at[part]
        )

    for part in range(2):
        pltpu.make_async_copy(ysend.at[part], yrecv.at[part], yr.at[part]).wait()
        ywide[...] = yrecv[part].astype(F32).reshape(seq_size * 32, LANE)
        for step in (2, 1, 3, 0):
            dest = lax.rem(node + step, NODES)
            for h in range(2):
                a = dest * 2 + h
                inner = ywide[pl.ds(a, width // 2, stride=8), :].T
                gate = gate_out[
                    pl.ds(pl.multiple_of(a * COLS, COLS), COLS), part * LANE : (part + 1) * LANE
                ]
                gsend[part, dest, h] = (gate.astype(F32) * inner).astype(BF16)
                if step:
                    remote(
                        gsend.at[part, dest, h],
                        grecv.at[part, node, core],
                        gs.at[part, step * 2 + h],
                        gr.at[part, node, core],
                        me,
                        dest * 2 + h,
                    ).start()
        own = gsend.at[part, node, core]
        pltpu.make_async_copy(own, grecv.at[part, node, core], gr.at[part, node, core]).start()
        remote(
            gsend.at[part, node, 1 - core],
            grecv.at[part, node, core],
            gs.at[part, 0],
            gr.at[part, node, core],
            me,
            mc + 1 - 2 * core,
        ).start()
        if part == 0:
            rest = weight.at[core, near, pl.ds(0, QUARTERS - 1)]
            pltpu.make_async_copy(rest, rest, wr.at[1]).wait()
            hand_over(1, near).start()
            pltpu.make_async_copy(rest, rest, er.at[0]).wait()
            hand_over(2, far).start()
    pass_across().wait_recv()
    pass_beside(1, across)

    def product(sources, n):
        lanes = slice(n * SPAN, (n + 1) * SPAN)
        rows = jnp.concatenate([grecv[p, w, k] for p, w in sources for k in range(2)], axis=1)
        block = jnp.concatenate(
            [
                weight[k, w, 2 * p : 2 * p + 2, :, lanes].reshape(LANE, SPAN)
                for p, w in sources
                for k in range(2)
            ]
        )
        return mm(rows, block)

    def arrive(part, which):
        for k in range(2):
            block = grecv.at[part, which, k]
            pltpu.make_async_copy(block, block, gr.at[part, which, k]).wait()

    arrive(0, node)
    arrive(1, node)
    hand_over(0, node).wait_recv()
    for n in range(SPANS):
        partial[n] = product([(0, node), (1, node)], n)
    hand_over(1, near).wait_recv()
    hand_over(2, far).wait_recv()
    for part in range(2):
        arrive(part, near)
        arrive(part, far)
        for n in range(SPANS):
            partial[n] += product([(part, near), (part, far)], n)
        if part == 0:
            pltpu.make_async_copy(rest, rest, er.at[1]).wait()
            hand_over(3, across).start()
    hand_over(3, across).wait_recv()
    arrive(0, across)
    arrive(1, across)
    for n in range(SPANS):
        lanes = slice(n * SPAN, (n + 1) * SPAN)
        out[:, lanes] = (partial[n] + product([(0, across), (1, across)], n)).astype(BF16)

    others = pl.ds(0, seq_size - 1)
    pltpu.make_async_copy(xsend.at[others], xrecv.at[others], xs).wait()
    for part in range(2):
        pltpu.make_async_copy(hsend.at[part, others], hrecv.at[part, others], hs.at[part]).wait()
    for part in range(2):
        pltpu.make_async_copy(ysend.at[part, others], yrecv.at[part, others], ys.at[part]).wait()
        for step in [0, 2, 3, 4, 5, 6, 7]:
            pltpu.make_async_copy(
                gsend.at[0, 0, 0], grecv.at[0, 0, 0], gs.at[part, step]
            ).wait()
    for slot, which in enumerate((node, near, far, across)):
        hand_over(slot, which).wait_send()
    pass_near(0).wait_send()
    pltpu.make_async_copy(rest, rest, ws.at[1]).wait()
    pass_pair().wait_send()
    pass_across().wait_send()
    for slot in range(2):
        pltpu.make_async_copy(rest, rest, es.at[slot]).wait()


def local(value, gate_in, gate_out, skip_weight, spectrum, out_weight):
    seq_size = lax.axis_size("seq")
    half_rows = 8 * seq_size
    row_count = 2 * half_rows
    width = CH * seq_size
    features = out_weight.shape[1]
    groups = seq_size // GROUP
    krows = GROUP * BAND
    mats = constants(seq_size)
    vmem = pl.BlockSpec(memory_space=pltpu.VMEM)
    smem = pl.BlockSpec(memory_space=pltpu.SMEM)
    hbm = pl.BlockSpec(memory_space=pl.ANY)
    dma = pltpu.SemaphoreType.DMA
    return pl.pallas_call(
        functools.partial(conv_kernel, seq_size),
        out_shape=jax.ShapeDtypeStruct((COLS, features), BF16),
        in_specs=[hbm, hbm, hbm, smem, hbm, hbm] + [hbm] * 5,
        out_specs=vmem,
        scratch_shapes=[
            *[pltpu.VMEM(m.shape, F32 if m.dtype == np.float32 else BF16) for m in mats],
            pltpu.VMEM((1024, width), BF16),
            pltpu.VMEM((1024, width), BF16),
            pltpu.VMEM((1024, width), BF16),
            pltpu.VMEM((2, BAND, COLS, width), F32),
            pltpu.VMEM((2, NODES, QUARTERS, width // QUARTERS, features), BF16),
            pltpu.VMEM((seq_size, 64, LANE), BF16),
            pltpu.VMEM((seq_size, 64, LANE), BF16),
            pltpu.VMEM((seq_size * 64, LANE), F32),
            pltpu.VMEM((half_rows, CH * LANE), BF16),
            pltpu.VMEM((BAND * width, LANE), F32),
            pltpu.VMEM((2, seq_size, CH * BAND, LANE), BF16),
            pltpu.VMEM((2, seq_size, CH * BAND, LANE), BF16),
            pltpu.VMEM((CH, row_count, 2 * LANE), F32),
            pltpu.VMEM((2 * krows, CH * LANE), BF16),
            pltpu.VMEM((half_rows, CH * LANE), F32),
            pltpu.VMEM((2, seq_size, 32, LANE), BF16),
            pltpu.VMEM((2, seq_size, 32, LANE), BF16),
            pltpu.VMEM((seq_size * 32, LANE), F32),
            pltpu.VMEM((2, NODES, 2, COLS, LANE), BF16),
            pltpu.VMEM((2, NODES, 2, COLS, LANE), BF16),
            pltpu.VMEM((SPANS, COLS, SPAN), F32),
            dma((9,)),
            dma((2,)),
            dma,
            dma,
            dma((2,)),
            dma((2, groups)),
            dma((2,)),
            dma((2,)),
            dma((2, 2 * NODES)),
            dma((2, NODES, 2)),
            dma((4,)),
            dma((4,)),
            dma((2,)),
            dma((2,)),
            dma((NODES,)),
            dma((NODES,)),
        ],
        compiler_params=pltpu.CompilerParams(
            collective_id=0, has_side_effects=True, vmem_limit_bytes=60 * 1024 * 1024
        ),
        name="long_conv",
    )(
        value,
        gate_in,
        gate_out,
        skip_weight,
        spectrum,
        out_weight.reshape(QUARTERS, width // QUARTERS, features),
        *[jnp.asarray(m) for m in mats],
    )


def solution(mesh):
    placed = (
        P("seq", "chan"),
        P("seq", "chan"),
        P("seq", "chan"),
        P("chan"),
        P(None, "seq", None, "chan"),
        P("chan", None),
    )
    return jax.shard_map(
        local, mesh=mesh, in_specs=placed, out_specs=P(("seq", "chan"), None), check_vma=False
    )
```

```python
import functools
import math

import jax
import jax.numpy as jnp
import ml_dtypes
import numpy as np
from jax import lax
from jax.experimental import pallas as pl
from jax.experimental.pallas import tpu as pltpu
from jax.sharding import PartitionSpec as P

COLS = 128
LANE = 128
CH = 8
BAND = 16
GROUP = 8
NODES = 4
QUARTERS = 4
SPANS, SPAN = 4, 512
MESH = pl.DeviceIdType.MESH
F32 = jnp.float32
BF16 = jnp.bfloat16


def two_terms(matrix):
    high = matrix.astype(np.float32).astype(ml_dtypes.bfloat16)
    low = (matrix - high.astype(np.float64)).astype(np.float32).astype(ml_dtypes.bfloat16)
    return np.stack([high, low])


def constants(seq_size):
    half_rows = 8 * seq_size
    row_count = 2 * half_rows
    padded_len = row_count * COLS
    k1 = np.arange(row_count)
    a = np.arange(half_rows)
    b = np.arange(COLS)
    row = 2.0 * np.pi / row_count * (np.outer(k1, a) % row_count)
    fwd_row = np.concatenate([np.cos(row), -np.sin(row)], axis=0)
    twist = 2.0 * np.pi / padded_len * (np.outer(k1, b) % padded_len)
    turn = np.stack([np.cos(twist), np.sin(twist)]).astype(np.float32)
    col = 2.0 * np.pi / COLS * (np.outer(b, b) % COLS)
    cos, sin = np.cos(col), np.sin(col)
    fwd_col = np.block([[cos, -sin], [sin, cos]])
    inv_col = np.block([[cos, sin], [-sin, cos]])
    groups = seq_size // min(GROUP, seq_size)
    back = row.T.reshape(half_rows, groups, -1)
    inv_row = np.concatenate([np.cos(back), -np.sin(back)], axis=2) / padded_len
    inv_row = np.ascontiguousarray(inv_row.transpose(1, 0, 2))
    return two_terms(fwd_row), turn, two_terms(fwd_col), two_terms(inv_col), two_terms(inv_row)


def mm(x, y):
    return jnp.dot(x, y, preferred_element_type=F32)


def conv_kernel(
    seq_size,
    value_hbm,
    gate_in_hbm,
    gate_out_hbm,
    skip,
    spectrum,
    weight_hbm,
    fwd_row_hbm,
    turn_hbm,
    fwd_col_hbm,
    inv_col_hbm,
    inv_row_hbm,
    out,
    fwd_row,
    turn,
    fwd_col,
    inv_col,
    inv_row,
    value,
    gate_in,
    gate_out,
    spec_buf,
    weight,
    xsend,
    xrecv,
    xwide,
    xgrid,
    hwide,
    hsend,
    hrecv,
    freq,
    back,
    total,
    ysend,
    yrecv,
    ywide,
    gsend,
    grecv,
    partial,
    load_sem,
    spec_sem,
    xs,
    xr,
    hs,
    hr,
    ys,
    yr,
    gs,
    gr,
    ws,
    wr,
    es,
    er,
    cs,
    cr,
    result,
    os,
):
    me = lax.axis_index("seq")
    mc = lax.axis_index("chan")
    half_rows = 8 * seq_size
    row_count = 2 * half_rows
    width = CH * seq_size
    members = GROUP
    groups = seq_size // members
    krows = members * BAND
    px, py, low = me // 8, lax.rem(me // 2, 4), lax.rem(me, 2)
    node, core = mc // 2, lax.rem(mc, 2)
    pair_chip = me + 1 - 2 * low
    near = lax.rem(node + 3 + 2 * low, NODES)
    far = lax.rem(node + 5 - 2 * low, NODES)
    across = lax.rem(node + 2, NODES)
    mine = lax.rem(px + 2 * py, QUARTERS)
    beside = [
        lax.rem(px + 1, 4) * 8 + py * 2 + low,
        lax.rem(px + 3, 4) * 8 + py * 2 + low,
        px * 8 + lax.rem(py + 1, 4) * 2 + low,
        px * 8 + lax.rem(py + 3, 4) * 2 + low,
    ]

    def remote(src, dst, send_sem, recv_sem, seq, chan):
        return pltpu.make_async_remote_copy(
            src_ref=src,
            dst_ref=dst,
            send_sem=send_sem,
            recv_sem=recv_sem,
            device_id=(seq, chan),
            device_id_type=MESH,
        )

    mixed_loads = [
        pltpu.make_async_copy(value_hbm, value, load_sem.at[6]),
        pltpu.make_async_copy(gate_in_hbm, gate_in, load_sem.at[7]),
    ]
    weight_load = pltpu.make_async_copy(weight_hbm, weight.at[core, node], load_sem.at[8])
    loads = [
        pltpu.make_async_copy(fwd_row_hbm, fwd_row, load_sem.at[0]),
        pltpu.make_async_copy(turn_hbm, turn, load_sem.at[1]),
        pltpu.make_async_copy(fwd_col_hbm, fwd_col, load_sem.at[2]),
        pltpu.make_async_copy(inv_col_hbm, inv_col, load_sem.at[3]),
        pltpu.make_async_copy(inv_row_hbm, inv_row, load_sem.at[4]),
        pltpu.make_async_copy(gate_out_hbm, gate_out, load_sem.at[5]),
    ]
    spec_loads = [
        pltpu.make_async_copy(spectrum.at[part], spec_buf.at[part], spec_sem.at[part])
        for part in range(2)
    ]
    for copy in mixed_loads + [weight_load] + spec_loads + loads:
        copy.start()

    barrier = pltpu.get_barrier_semaphore()

    def greet(seq, chan):
        pl.semaphore_signal(barrier, inc=1, device_id=(seq, chan), device_id_type=MESH)

    def greet_seq(d, _):
        greet(lax.rem(me + d, seq_size), mc)
        return 0

    lax.fori_loop(1, seq_size, greet_seq, 0)
    greet(pair_chip, near * 2 + core)
    for step in range(1, 2 * NODES):
        greet(me, lax.rem(mc + step, 2 * NODES))

    def exchange(src_of, dst, send_sem, recv_sem):
        pltpu.make_async_copy(src_of(me), dst, recv_sem).start()

        def send(d, _):
            peer = (
                lax.rem(px + d // 8, 4) * 8
                + lax.rem(py + lax.rem(d // 2, 4), 4) * 2
                + lax.rem(low + d, 2)
            )
            remote(src_of(peer), dst, send_sem, recv_sem, peer, mc).start()
            return 0

        lax.fori_loop(1, seq_size, send, 0)

    def pass_near(step):
        block = weight.at[core, node, lax.rem(mine + step, QUARTERS)]
        sem = min(step, 1)
        return remote(block, block, ws.at[sem], wr.at[sem], pair_chip, near * 2 + core)

    def pass_pair():
        block = weight.at[core, near, mine]
        return remote(block, block, ws.at[2], wr.at[2], pair_chip, mc)

    def pass_across():
        block = weight.at[core, far, mine]
        return remote(block, block, ws.at[3], wr.at[3], pair_chip, near * 2 + core)

    def pass_beside(slot, which):
        for e, seq in enumerate(beside):
            rows = pl.ds(0, 64) if e < 2 else pl.ds((e - 2) * 32, 32)
            block = weight.at[core, which, mine, rows]
            remote(block, block, es.at[slot], er.at[slot], seq, mc).start()

    def hand_over(slot, which):
        block = weight.at[core, which]
        return remote(block, block, cs.at[slot], cr.at[slot], me, mc + 1 - 2 * core)

    def channel(dest, c):
        return (c // 4) * (width // 2) + dest * 4 + c % 4

    for copy in mixed_loads:
        copy.wait()
    for a in range(8):
        rows = slice(a * COLS, (a + 1) * COLS)
        mixed = (gate_in[rows, :].astype(F32) * value[rows, :].astype(F32)).astype(BF16)
        xwide[a * width : (a + 1) * width, :] = mixed.astype(F32).T

    def pack_input(dest, _):
        for pair in range(CH // 2):
            rows = [
                xwide[pl.ds(channel(dest, c), 8, stride=width), :] for c in (2 * pair, 2 * pair + 1)
            ]
            xsend[dest, pair * 16 : (pair + 1) * 16, :] = jnp.concatenate(rows).astype(BF16)
        return 0

    lax.fori_loop(0, seq_size, pack_input, 0)

    weight_load.wait()
    pl.semaphore_wait(barrier, seq_size - 1 + 2 * NODES)
    pass_near(0).start()
    exchange(lambda peer: xsend.at[peer], xrecv.at[me], xs, xr)
    for step in range(1, QUARTERS):
        pass_near(step).start()
    hand_over(0, node).start()

    for part in range(2):
        spec_loads[part].wait()

        def turn_row(k, _):
            start = pl.multiple_of(k * width, width)
            hwide[pl.ds(start, width), :] = spec_buf[part, k].T
            return 0

        lax.fori_loop(0, BAND, turn_row, 0)

        def pack(dest, _):
            for c in range(CH):
                rows = hwide[pl.ds(channel(dest, c), BAND, stride=width), :]
                hsend[part, dest, c * BAND : (c + 1) * BAND, :] = rows.astype(BF16)
            return 0

        lax.fori_loop(0, seq_size, pack, 0)
        exchange(
            lambda peer: hsend.at[part, peer],
            hrecv.at[part, me],
            hs.at[part],
            hr.at[part, px],
        )
        if part == 0:
            pass_near(0).wait_recv()
            pass_pair().start()

    for copy in loads:
        copy.wait()
    pltpu.make_async_copy(xsend, xrecv, xr).wait()
    for c in range(CH):
        pair = xrecv[:, c // 2 * 16 : c // 2 * 16 + 16, :].astype(F32)
        rows = pair[:, c % 2 * 8 : c % 2 * 8 + 8, :].reshape(half_rows, LANE)
        xgrid[:, c * LANE : (c + 1) * LANE] = rows.astype(BF16)
    pass_pair().wait_recv()
    pass_across().start()
    pass_beside(0, far)

    def forward(g, _):
        rows = pl.ds(pl.multiple_of(g * krows, krows), krows)
        rows_im = pl.ds(pl.multiple_of(row_count + g * krows, krows), krows)
        cos, sin = turn[0, rows, :], turn[1, rows, :]
        for pair in range(CH // 2):
            x = xgrid[:, pair * 256 : (pair + 1) * 256]
            re = mm(fwd_row[0, rows, :], x) + mm(fwd_row[1, rows, :], x)
            im = mm(fwd_row[0, rows_im, :], x) + mm(fwd_row[1, rows_im, :], x)
            for h in range(2):
                r = re[:, h * LANE : (h + 1) * LANE]
                i = im[:, h * LANE : (h + 1) * LANE]
                turned = jnp.concatenate([r * cos + i * sin, i * cos - r * sin], axis=1)
                high = turned.astype(BF16)
                rest = (turned - high.astype(F32)).astype(BF16)
                freq[2 * pair + h, rows, :] = (
                    mm(high, fwd_col[0]) + mm(high, fwd_col[1]) + mm(rest, fwd_col[0])
                )
        return 0

    lax.fori_loop(0, groups, forward, 0)
    total[...] = jnp.zeros_like(total)

    def inverse(step, channels):
        g = lax.rem(px + groups - step, groups)
        members_at = pl.ds(pl.multiple_of(g * members, members), members)
        if 0 in channels:
            for part in range(2):
                block = hrecv.at[part, members_at]
                pltpu.make_async_copy(hsend.at[part, members_at], block, hr.at[part, g]).wait()
        rows = pl.ds(pl.multiple_of(g * krows, krows), krows)
        cos, sin = turn[0, rows, :], turn[1, rows, :]
        for c in channels:
            band = slice(c * BAND, (c + 1) * BAND)
            h_re = hrecv[0, members_at, band, :].astype(F32).reshape(krows, LANE)
            h_im = hrecv[1, members_at, band, :].astype(F32).reshape(krows, LANE)
            f_re, f_im = freq[c, rows, :LANE], freq[c, rows, LANE:]
            prod = jnp.concatenate([f_re * h_re - f_im * h_im, f_re * h_im + f_im * h_re], axis=1)
            prod = prod.astype(BF16)
            grid = mm(prod, inv_col[0]) + mm(prod, inv_col[1])
            b_re, b_im = grid[:, :LANE], grid[:, LANE:]
            lanes = slice(c * LANE, (c + 1) * LANE)
            back[:krows, lanes] = (b_re * cos - b_im * sin).astype(BF16)
            back[krows:, lanes] = (b_re * sin + b_im * cos).astype(BF16)
        for pair in range(channels[0] // 2, channels[-1] // 2 + 1):
            lanes = slice(pair * 256, (pair + 1) * 256)
            total[:, lanes] += mm(inv_row[0, g], back[:, lanes]) + mm(inv_row[1, g], back[:, lanes])

    def inverse_all(step, _):
        inverse(step, range(CH))
        return 0

    lax.fori_loop(0, groups - 1, inverse_all, 0)

    for part in range(2):
        inverse(groups - 1, range(part * 4, part * 4 + 4))
        for pair in range(2):
            halves = []
            for c in (part * 4 + 2 * pair, part * 4 + 2 * pair + 1):
                lanes = slice(c * LANE, (c + 1) * LANE)
                direct = skip[channel(me, c)] * xgrid[:, lanes].astype(F32)
                halves.append((total[:, lanes] + direct).reshape(seq_size, 8, LANE))
            rows = slice(pair * 16, (pair + 1) * 16)
            ysend[part, :, rows, :] = jnp.concatenate(halves, axis=1).astype(BF16)
        exchange(
            lambda peer: ysend.at[part, peer], yrecv.at[part, me], ys.at[part], yr.at[part]
        )

    for part in range(2):
        pltpu.make_async_copy(ysend.at[part], yrecv.at[part], yr.at[part]).wait()
        ywide[...] = yrecv[part].astype(F32).reshape(seq_size * 32, LANE)
        for step in (2, 1, 3, 0):
            dest = lax.rem(node + step, NODES)
            for h in range(2):
                a = dest * 2 + h
                inner = ywide[pl.ds(a, width // 2, stride=8), :].T
                gate = gate_out[
                    pl.ds(pl.multiple_of(a * COLS, COLS), COLS), part * LANE : (part + 1) * LANE
                ]
                gsend[part, dest, h] = (gate.astype(F32) * inner).astype(BF16)
                if step:
                    remote(
                        gsend.at[part, dest, h],
                        grecv.at[part, node, core],
                        gs.at[part, step * 2 + h],
                        gr.at[part, node, core],
                        me,
                        dest * 2 + h,
                    ).start()
        own = gsend.at[part, node, core]
        pltpu.make_async_copy(own, grecv.at[part, node, core], gr.at[part, node, core]).start()
        remote(
            gsend.at[part, node, 1 - core],
            grecv.at[part, node, core],
            gs.at[part, 0],
            gr.at[part, node, core],
            me,
            mc + 1 - 2 * core,
        ).start()
        if part == 0:
            rest = weight.at[core, near, pl.ds(0, QUARTERS - 1)]
            pltpu.make_async_copy(rest, rest, wr.at[1]).wait()
            hand_over(1, near).start()
            pltpu.make_async_copy(rest, rest, er.at[0]).wait()
            hand_over(2, far).start()
            pass_across().wait_recv()
            pass_beside(1, across)

    def product(sources, n):
        lanes = slice(n * SPAN, (n + 1) * SPAN)
        rows = jnp.concatenate([grecv[p, w, k] for p, w in sources for k in range(2)], axis=1)
        block = jnp.concatenate(
            [
                weight[k, w, 2 * p : 2 * p + 2, :, lanes].reshape(LANE, SPAN)
                for p, w in sources
                for k in range(2)
            ]
        )
        return mm(rows, block)

    def arrive(part, which):
        for k in range(2):
            block = grecv.at[part, which, k]
            pltpu.make_async_copy(block, block, gr.at[part, which, k]).wait()

    arrive(0, node)
    arrive(1, node)
    hand_over(0, node).wait_recv()
    for n in range(SPANS):
        partial[n] = product([(0, node), (1, node)], n)
    hand_over(1, near).wait_recv()
    hand_over(2, far).wait_recv()
    arrive(0, near)
    arrive(0, far)
    for n in range(SPANS):
        partial[n] += product([(0, near), (0, far)], n)
    pltpu.make_async_copy(rest, rest, er.at[1]).wait()
    hand_over(3, across).start()
    arrive(0, across)
    hand_over(3, across).wait_recv()
    for n in range(SPANS):
        partial[n] += product([(0, across)], n)
    for which in (near, far):
        arrive(1, which)
        for n in range(SPANS):
            partial[n] += product([(1, which)], n)
    arrive(1, across)
    for n in range(SPANS):
        lanes = slice(n * SPAN, (n + 1) * SPAN)
        result[:, lanes] = (partial[n] + product([(1, across)], n)).astype(BF16)
        pltpu.make_async_copy(result.at[:, lanes], out.at[:, lanes], os.at[n]).start()
    for n in range(SPANS):
        lanes = slice(n * SPAN, (n + 1) * SPAN)
        pltpu.make_async_copy(result.at[:, lanes], out.at[:, lanes], os.at[n]).wait()

    others = pl.ds(0, seq_size - 1)
    pltpu.make_async_copy(xsend.at[others], xrecv.at[others], xs).wait()
    for part in range(2):
        pltpu.make_async_copy(hsend.at[part, others], hrecv.at[part, others], hs.at[part]).wait()
    for part in range(2):
        pltpu.make_async_copy(ysend.at[part, others], yrecv.at[part, others], ys.at[part]).wait()
        for step in [0, 2, 3, 4, 5, 6, 7]:
            pltpu.make_async_copy(
                gsend.at[0, 0, 0], grecv.at[0, 0, 0], gs.at[part, step]
            ).wait()
    for slot, which in enumerate((node, near, far, across)):
        hand_over(slot, which).wait_send()
    pass_near(0).wait_send()
    pltpu.make_async_copy(rest, rest, ws.at[1]).wait()
    pass_pair().wait_send()
    pass_across().wait_send()
    for slot in range(2):
        pltpu.make_async_copy(rest, rest, es.at[slot]).wait()


def local(value, gate_in, gate_out, skip_weight, spectrum, out_weight):
    seq_size = lax.axis_size("seq")
    half_rows = 8 * seq_size
    row_count = 2 * half_rows
    width = CH * seq_size
    features = out_weight.shape[1]
    groups = seq_size // GROUP
    krows = GROUP * BAND
    mats = constants(seq_size)
    smem = pl.BlockSpec(memory_space=pltpu.SMEM)
    hbm = pl.BlockSpec(memory_space=pl.ANY)
    dma = pltpu.SemaphoreType.DMA
    return pl.pallas_call(
        functools.partial(conv_kernel, seq_size),
        out_shape=jax.ShapeDtypeStruct((COLS, features), BF16),
        in_specs=[hbm, hbm, hbm, smem, hbm, hbm] + [hbm] * 5,
        out_specs=hbm,
        scratch_shapes=[
            *[pltpu.VMEM(m.shape, F32 if m.dtype == np.float32 else BF16) for m in mats],
            pltpu.VMEM((1024, width), BF16),
            pltpu.VMEM((1024, width), BF16),
            pltpu.VMEM((1024, width), BF16),
            pltpu.VMEM((2, BAND, COLS, width), F32),
            pltpu.VMEM((2, NODES, QUARTERS, width // QUARTERS, features), BF16),
            pltpu.VMEM((seq_size, 64, LANE), BF16),
            pltpu.VMEM((seq_size, 64, LANE), BF16),
            pltpu.VMEM((seq_size * 64, LANE), F32),
            pltpu.VMEM((half_rows, CH * LANE), BF16),
            pltpu.VMEM((BAND * width, LANE), F32),
            pltpu.VMEM((2, seq_size, CH * BAND, LANE), BF16),
            pltpu.VMEM((2, seq_size, CH * BAND, LANE), BF16),
            pltpu.VMEM((CH, row_count, 2 * LANE), F32),
            pltpu.VMEM((2 * krows, CH * LANE), BF16),
            pltpu.VMEM((half_rows, CH * LANE), F32),
            pltpu.VMEM((2, seq_size, 32, LANE), BF16),
            pltpu.VMEM((2, seq_size, 32, LANE), BF16),
            pltpu.VMEM((seq_size * 32, LANE), F32),
            pltpu.VMEM((2, NODES, 2, COLS, LANE), BF16),
            pltpu.VMEM((2, NODES, 2, COLS, LANE), BF16),
            pltpu.VMEM((SPANS, COLS, SPAN), F32),
            dma((9,)),
            dma((2,)),
            dma,
            dma,
            dma((2,)),
            dma((2, groups)),
            dma((2,)),
            dma((2,)),
            dma((2, 2 * NODES)),
            dma((2, NODES, 2)),
            dma((4,)),
            dma((4,)),
            dma((2,)),
            dma((2,)),
            dma((NODES,)),
            dma((NODES,)),
            pltpu.VMEM((COLS, features), BF16),
            dma((SPANS,)),
        ],
        compiler_params=pltpu.CompilerParams(
            collective_id=0, has_side_effects=True, vmem_limit_bytes=60 * 1024 * 1024
        ),
        name="long_conv",
    )(
        value,
        gate_in,
        gate_out,
        skip_weight,
        spectrum,
        out_weight.reshape(QUARTERS, width // QUARTERS, features),
        *[jnp.asarray(m) for m in mats],
    )


def solution(mesh):
    placed = (
        P("seq", "chan"),
        P("seq", "chan"),
        P("seq", "chan"),
        P("chan"),
        P(None, "seq", None, "chan"),
        P("chan", None),
    )
    return jax.shard_map(
        local, mesh=mesh, in_specs=placed, out_specs=P(("seq", "chan"), None), check_vma=False
    )
```

```python
import functools
import math

import jax
import jax.numpy as jnp
import ml_dtypes
import numpy as np
from jax import lax
from jax.experimental import pallas as pl
from jax.experimental.pallas import tpu as pltpu
from jax.sharding import PartitionSpec as P

COLS = 128
LANE = 128
CH = 8
BAND = 16
GROUP = 8
NODES = 4
QUARTERS = 4
SPANS, SPAN = 4, 512
MESH = pl.DeviceIdType.MESH
F32 = jnp.float32
BF16 = jnp.bfloat16


def two_terms(matrix):
    high = matrix.astype(np.float32).astype(ml_dtypes.bfloat16)
    low = (matrix - high.astype(np.float64)).astype(np.float32).astype(ml_dtypes.bfloat16)
    return np.stack([high, low])


def constants(seq_size):
    half_rows = 8 * seq_size
    row_count = 2 * half_rows
    padded_len = row_count * COLS
    k1 = np.arange(row_count)
    a = np.arange(half_rows)
    b = np.arange(COLS)
    row = 2.0 * np.pi / row_count * (np.outer(k1, a) % row_count)
    fwd_row = np.concatenate([np.cos(row), -np.sin(row)], axis=0)
    twist = 2.0 * np.pi / padded_len * (np.outer(k1, b) % padded_len)
    turn = np.stack([np.cos(twist), np.sin(twist)]).astype(np.float32)
    col = 2.0 * np.pi / COLS * (np.outer(b, b) % COLS)
    cos, sin = np.cos(col), np.sin(col)
    fwd_col = np.block([[cos, -sin], [sin, cos]])
    inv_col = np.block([[cos, sin], [-sin, cos]])
    groups = seq_size // min(GROUP, seq_size)
    back = row.T.reshape(half_rows, groups, -1)
    inv_row = np.concatenate([np.cos(back), -np.sin(back)], axis=2) / padded_len
    inv_row = np.ascontiguousarray(inv_row.transpose(1, 0, 2))
    return two_terms(fwd_row), turn, two_terms(fwd_col), two_terms(inv_col), two_terms(inv_row)


def mm(x, y):
    return jnp.dot(x, y, preferred_element_type=F32)


def conv_kernel(
    seq_size,
    value_hbm,
    gate_in_hbm,
    gate_out_hbm,
    skip,
    spectrum,
    weight_hbm,
    fwd_row_hbm,
    turn_hbm,
    fwd_col_hbm,
    inv_col_hbm,
    inv_row_hbm,
    out,
    fwd_row,
    turn,
    fwd_col,
    inv_col,
    inv_row,
    value,
    gate_in,
    gate_out,
    spec_buf,
    weight,
    xsend,
    xrecv,
    xwide,
    xgrid,
    hwide,
    hsend,
    hrecv,
    freq,
    back,
    total,
    ysend,
    yrecv,
    ywide,
    gsend,
    grecv,
    partial,
    load_sem,
    spec_sem,
    xs,
    xr,
    hs,
    hr,
    ys,
    yr,
    gs,
    gr,
    ws,
    wr,
    es,
    er,
    cs,
    cr,
    result,
    os,
):
    me = lax.axis_index("seq")
    mc = lax.axis_index("chan")
    half_rows = 8 * seq_size
    row_count = 2 * half_rows
    width = CH * seq_size
    members = GROUP
    groups = seq_size // members
    krows = members * BAND
    px, py, low = me // 8, lax.rem(me // 2, 4), lax.rem(me, 2)
    node, core = mc // 2, lax.rem(mc, 2)
    pair_chip = me + 1 - 2 * low
    near = lax.rem(node + 3 + 2 * low, NODES)
    far = lax.rem(node + 5 - 2 * low, NODES)
    across = lax.rem(node + 2, NODES)
    mine = lax.rem(px + 2 * py, QUARTERS)
    beside = [
        lax.rem(px + 1, 4) * 8 + py * 2 + low,
        lax.rem(px + 3, 4) * 8 + py * 2 + low,
        px * 8 + lax.rem(py + 1, 4) * 2 + low,
        px * 8 + lax.rem(py + 3, 4) * 2 + low,
    ]

    def remote(src, dst, send_sem, recv_sem, seq, chan):
        return pltpu.make_async_remote_copy(
            src_ref=src,
            dst_ref=dst,
            send_sem=send_sem,
            recv_sem=recv_sem,
            device_id=(seq, chan),
            device_id_type=MESH,
        )

    mixed_loads = [
        pltpu.make_async_copy(value_hbm, value, load_sem.at[6]),
        pltpu.make_async_copy(gate_in_hbm, gate_in, load_sem.at[7]),
    ]
    weight_load = pltpu.make_async_copy(weight_hbm, weight.at[core, node], load_sem.at[8])
    loads = [
        pltpu.make_async_copy(fwd_row_hbm, fwd_row, load_sem.at[0]),
        pltpu.make_async_copy(turn_hbm, turn, load_sem.at[1]),
        pltpu.make_async_copy(fwd_col_hbm, fwd_col, load_sem.at[2]),
        pltpu.make_async_copy(inv_col_hbm, inv_col, load_sem.at[3]),
        pltpu.make_async_copy(inv_row_hbm, inv_row, load_sem.at[4]),
        pltpu.make_async_copy(gate_out_hbm, gate_out, load_sem.at[5]),
    ]
    spec_loads = [
        pltpu.make_async_copy(spectrum.at[part], spec_buf.at[part], spec_sem.at[part])
        for part in range(2)
    ]
    for copy in mixed_loads:
        copy.start()

    barrier = pltpu.get_barrier_semaphore()

    def greet(seq, chan):
        pl.semaphore_signal(barrier, inc=1, device_id=(seq, chan), device_id_type=MESH)

    def greet_seq(d, _):
        greet(lax.rem(me + d, seq_size), mc)
        return 0

    lax.fori_loop(1, seq_size, greet_seq, 0)
    greet(pair_chip, near * 2 + core)
    for step in range(1, 2 * NODES):
        greet(me, lax.rem(mc + step, 2 * NODES))

    def exchange(src_of, dst, send_sem, recv_sem):
        pltpu.make_async_copy(src_of(me), dst, recv_sem).start()

        def send(d, _):
            peer = (
                lax.rem(px + d // 8, 4) * 8
                + lax.rem(py + lax.rem(d // 2, 4), 4) * 2
                + lax.rem(low + d, 2)
            )
            remote(src_of(peer), dst, send_sem, recv_sem, peer, mc).start()
            return 0

        lax.fori_loop(1, seq_size, send, 0)

    def pass_near(step):
        block = weight.at[core, node, lax.rem(mine + step, QUARTERS)]
        sem = min(step, 1)
        return remote(block, block, ws.at[sem], wr.at[sem], pair_chip, near * 2 + core)

    def pass_pair():
        block = weight.at[core, near, mine]
        return remote(block, block, ws.at[2], wr.at[2], pair_chip, mc)

    def pass_across():
        block = weight.at[core, far, mine]
        return remote(block, block, ws.at[3], wr.at[3], pair_chip, near * 2 + core)

    def pass_beside(slot, which):
        for e, seq in enumerate(beside):
            rows = pl.ds(0, 64) if e < 2 else pl.ds((e - 2) * 32, 32)
            block = weight.at[core, which, mine, rows]
            remote(block, block, es.at[slot], er.at[slot], seq, mc).start()

    def hand_over(slot, which):
        block = weight.at[core, which]
        return remote(block, block, cs.at[slot], cr.at[slot], me, mc + 1 - 2 * core)

    def channel(dest, c):
        return (c // 4) * (width // 2) + dest * 4 + c % 4

    for copy in mixed_loads:
        copy.wait()
    for copy in [weight_load] + spec_loads + loads:
        copy.start()
    for a in range(8):
        rows = slice(a * COLS, (a + 1) * COLS)
        mixed = (gate_in[rows, :].astype(F32) * value[rows, :].astype(F32)).astype(BF16)
        xwide[a * width : (a + 1) * width, :] = mixed.astype(F32).T

    def pack_input(dest, _):
        for pair in range(CH // 2):
            rows = [
                xwide[pl.ds(channel(dest, c), 8, stride=width), :] for c in (2 * pair, 2 * pair + 1)
            ]
            xsend[dest, pair * 16 : (pair + 1) * 16, :] = jnp.concatenate(rows).astype(BF16)
        return 0

    lax.fori_loop(0, seq_size, pack_input, 0)

    weight_load.wait()
    pl.semaphore_wait(barrier, seq_size - 1 + 2 * NODES)
    pass_near(0).start()
    exchange(lambda peer: xsend.at[peer], xrecv.at[me], xs, xr)
    for step in range(1, QUARTERS):
        pass_near(step).start()
    hand_over(0, node).start()

    for part in range(2):
        spec_loads[part].wait()

        def turn_row(k, _):
            start = pl.multiple_of(k * width, width)
            hwide[pl.ds(start, width), :] = spec_buf[part, k].T
            return 0

        lax.fori_loop(0, BAND, turn_row, 0)

        def pack(dest, _):
            for c in range(CH):
                rows = hwide[pl.ds(channel(dest, c), BAND, stride=width), :]
                hsend[part, dest, c * BAND : (c + 1) * BAND, :] = rows.astype(BF16)
            return 0

        lax.fori_loop(0, seq_size, pack, 0)
        exchange(
            lambda peer: hsend.at[part, peer],
            hrecv.at[part, me],
            hs.at[part],
            hr.at[part, px],
        )
        if part == 0:
            pass_near(0).wait_recv()
            pass_pair().start()

    for copy in loads:
        copy.wait()
    pltpu.make_async_copy(xsend, xrecv, xr).wait()
    for c in range(CH):
        pair = xrecv[:, c // 2 * 16 : c // 2 * 16 + 16, :].astype(F32)
        rows = pair[:, c % 2 * 8 : c % 2 * 8 + 8, :].reshape(half_rows, LANE)
        xgrid[:, c * LANE : (c + 1) * LANE] = rows.astype(BF16)
    pass_pair().wait_recv()
    pass_across().start()
    pass_beside(0, far)

    def forward(g, _):
        rows = pl.ds(pl.multiple_of(g * krows, krows), krows)
        rows_im = pl.ds(pl.multiple_of(row_count + g * krows, krows), krows)
        cos, sin = turn[0, rows, :], turn[1, rows, :]
        for pair in range(CH // 2):
            x = xgrid[:, pair * 256 : (pair + 1) * 256]
            re = mm(fwd_row[0, rows, :], x) + mm(fwd_row[1, rows, :], x)
            im = mm(fwd_row[0, rows_im, :], x) + mm(fwd_row[1, rows_im, :], x)
            for h in range(2):
                r = re[:, h * LANE : (h + 1) * LANE]
                i = im[:, h * LANE : (h + 1) * LANE]
                turned = jnp.concatenate([r * cos + i * sin, i * cos - r * sin], axis=1)
                high = turned.astype(BF16)
                rest = (turned - high.astype(F32)).astype(BF16)
                freq[2 * pair + h, rows, :] = (
                    mm(high, fwd_col[0]) + mm(high, fwd_col[1]) + mm(rest, fwd_col[0])
                )
        return 0

    lax.fori_loop(0, groups, forward, 0)
    total[...] = jnp.zeros_like(total)

    def inverse(step, channels):
        g = lax.rem(px + groups - step, groups)
        members_at = pl.ds(pl.multiple_of(g * members, members), members)
        if 0 in channels:
            for part in range(2):
                block = hrecv.at[part, members_at]
                pltpu.make_async_copy(hsend.at[part, members_at], block, hr.at[part, g]).wait()
        rows = pl.ds(pl.multiple_of(g * krows, krows), krows)
        cos, sin = turn[0, rows, :], turn[1, rows, :]
        for c in channels:
            band = slice(c * BAND, (c + 1) * BAND)
            h_re = hrecv[0, members_at, band, :].astype(F32).reshape(krows, LANE)
            h_im = hrecv[1, members_at, band, :].astype(F32).reshape(krows, LANE)
            f_re, f_im = freq[c, rows, :LANE], freq[c, rows, LANE:]
            prod = jnp.concatenate([f_re * h_re - f_im * h_im, f_re * h_im + f_im * h_re], axis=1)
            prod = prod.astype(BF16)
            grid = mm(prod, inv_col[0]) + mm(prod, inv_col[1])
            b_re, b_im = grid[:, :LANE], grid[:, LANE:]
            lanes = slice(c * LANE, (c + 1) * LANE)
            back[:krows, lanes] = (b_re * cos - b_im * sin).astype(BF16)
            back[krows:, lanes] = (b_re * sin + b_im * cos).astype(BF16)
        for pair in range(channels[0] // 2, channels[-1] // 2 + 1):
            lanes = slice(pair * 256, (pair + 1) * 256)
            total[:, lanes] += mm(inv_row[0, g], back[:, lanes]) + mm(inv_row[1, g], back[:, lanes])

    def inverse_all(step, _):
        inverse(step, range(CH))
        return 0

    lax.fori_loop(0, groups - 1, inverse_all, 0)

    for part in range(2):
        inverse(groups - 1, range(part * 4, part * 4 + 4))
        for pair in range(2):
            halves = []
            for c in (part * 4 + 2 * pair, part * 4 + 2 * pair + 1):
                lanes = slice(c * LANE, (c + 1) * LANE)
                direct = skip[channel(me, c)] * xgrid[:, lanes].astype(F32)
                halves.append((total[:, lanes] + direct).reshape(seq_size, 8, LANE))
            rows = slice(pair * 16, (pair + 1) * 16)
            ysend[part, :, rows, :] = jnp.concatenate(halves, axis=1).astype(BF16)
        exchange(
            lambda peer: ysend.at[part, peer], yrecv.at[part, me], ys.at[part], yr.at[part]
        )

    rest = weight.at[core, near, pl.ds(0, QUARTERS - 1)]
    for part in range(2):
        pltpu.make_async_copy(ysend.at[part], yrecv.at[part], yr.at[part]).wait()
        ywide[: seq_size * 32, :] = yrecv[part].astype(F32).reshape(seq_size * 32, LANE)
        for step in (1, 3, 2, 0):
            dest = lax.rem(node + step, NODES)
            for h in range(2):
                a = dest * 2 + h
                inner = ywide[pl.ds(a, width // 2, stride=8), :].T
                gate = gate_out[
                    pl.ds(pl.multiple_of(a * COLS, COLS), COLS), part * LANE : (part + 1) * LANE
                ]
                gsend[part, dest, h] = (gate.astype(F32) * inner).astype(BF16)
                if step:
                    remote(
                        gsend.at[part, dest, h],
                        grecv.at[part, node, core],
                        gs.at[part, step * 2 + h],
                        gr.at[part, node, core],
                        me,
                        dest * 2 + h,
                    ).start()
        own = gsend.at[part, node, core]
        pltpu.make_async_copy(own, grecv.at[part, node, core], gr.at[part, node, core]).start()
        remote(
            gsend.at[part, node, 1 - core],
            grecv.at[part, node, core],
            gs.at[part, 0],
            gr.at[part, node, core],
            me,
            mc + 1 - 2 * core,
        ).start()
        if part == 0:
            pltpu.make_async_copy(rest, rest, wr.at[1]).wait()
            hand_over(1, near).start()
            pass_across().wait_recv()
            pass_beside(1, across)

    pltpu.make_async_copy(rest, rest, er.at[0]).wait()
    hand_over(2, far).start()

    def product(sources, n):
        lanes = slice(n * SPAN, (n + 1) * SPAN)
        rows = jnp.concatenate([grecv[p, w, k] for p, w in sources for k in range(2)], axis=1)
        block = jnp.concatenate(
            [
                weight[k, w, 2 * p : 2 * p + 2, :, lanes].reshape(LANE, SPAN)
                for p, w in sources
                for k in range(2)
            ]
        )
        return mm(rows, block)

    def arrive(part, which):
        for k in range(2):
            block = grecv.at[part, which, k]
            pltpu.make_async_copy(block, block, gr.at[part, which, k]).wait()

    arrive(0, node)
    arrive(1, node)
    hand_over(0, node).wait_recv()
    for n in range(SPANS):
        partial[n] = product([(0, node), (1, node)], n)
    hand_over(1, near).wait_recv()
    hand_over(2, far).wait_recv()
    arrive(0, near)
    arrive(0, far)
    for n in range(SPANS):
        partial[n] += product([(0, near), (0, far)], n)
    pltpu.make_async_copy(rest, rest, er.at[1]).wait()
    hand_over(3, across).start()
    arrive(0, across)
    hand_over(3, across).wait_recv()
    for n in range(SPANS):
        partial[n] += product([(0, across)], n)
    for which in (near, far):
        arrive(1, which)
        for n in range(SPANS):
            partial[n] += product([(1, which)], n)
    arrive(1, across)
    for n in range(SPANS):
        lanes = slice(n * SPAN, (n + 1) * SPAN)
        result[:, lanes] = (partial[n] + product([(1, across)], n)).astype(BF16)
        pltpu.make_async_copy(result.at[:, lanes], out.at[:, lanes], os.at[n]).start()
    for n in range(SPANS):
        lanes = slice(n * SPAN, (n + 1) * SPAN)
        pltpu.make_async_copy(result.at[:, lanes], out.at[:, lanes], os.at[n]).wait()

    others = pl.ds(0, seq_size - 1)
    pltpu.make_async_copy(xsend.at[others], xrecv.at[others], xs).wait()
    for part in range(2):
        pltpu.make_async_copy(hsend.at[part, others], hrecv.at[part, others], hs.at[part]).wait()
    for part in range(2):
        pltpu.make_async_copy(ysend.at[part, others], yrecv.at[part, others], ys.at[part]).wait()
        for step in [0, 2, 3, 4, 5, 6, 7]:
            pltpu.make_async_copy(
                gsend.at[0, 0, 0], grecv.at[0, 0, 0], gs.at[part, step]
            ).wait()
    for slot, which in enumerate((node, near, far, across)):
        hand_over(slot, which).wait_send()
    pass_near(0).wait_send()
    pltpu.make_async_copy(rest, rest, ws.at[1]).wait()
    pass_pair().wait_send()
    pass_across().wait_send()
    for slot in range(2):
        pltpu.make_async_copy(rest, rest, es.at[slot]).wait()


def local(value, gate_in, gate_out, skip_weight, spectrum, out_weight):
    seq_size = lax.axis_size("seq")
    half_rows = 8 * seq_size
    row_count = 2 * half_rows
    width = CH * seq_size
    features = out_weight.shape[1]
    groups = seq_size // GROUP
    krows = GROUP * BAND
    mats = constants(seq_size)
    smem = pl.BlockSpec(memory_space=pltpu.SMEM)
    hbm = pl.BlockSpec(memory_space=pl.ANY)
    dma = pltpu.SemaphoreType.DMA
    return pl.pallas_call(
        functools.partial(conv_kernel, seq_size),
        out_shape=jax.ShapeDtypeStruct((COLS, features), BF16),
        in_specs=[hbm, hbm, hbm, smem, hbm, hbm] + [hbm] * 5,
        out_specs=hbm,
        scratch_shapes=[
            *[pltpu.VMEM(m.shape, F32 if m.dtype == np.float32 else BF16) for m in mats],
            pltpu.VMEM((1024, width), BF16),
            pltpu.VMEM((1024, width), BF16),
            pltpu.VMEM((1024, width), BF16),
            pltpu.VMEM((2, BAND, COLS, width), F32),
            pltpu.VMEM((2, NODES, QUARTERS, width // QUARTERS, features), BF16),
            pltpu.VMEM((seq_size, 64, LANE), BF16),
            pltpu.VMEM((seq_size, 64, LANE), BF16),
            pltpu.VMEM((seq_size * 64 + width, LANE), F32),
            pltpu.VMEM((half_rows, CH * LANE), BF16),
            pltpu.VMEM(((BAND + 1) * width, LANE), F32),
            pltpu.VMEM((2, seq_size, CH * BAND, LANE), BF16),
            pltpu.VMEM((2, seq_size, CH * BAND, LANE), BF16),
            pltpu.VMEM((CH, row_count, 2 * LANE), F32),
            pltpu.VMEM((2 * krows, CH * LANE), BF16),
            pltpu.VMEM((half_rows, CH * LANE), F32),
            pltpu.VMEM((2, seq_size, 32, LANE), BF16),
            pltpu.VMEM((2, seq_size, 32, LANE), BF16),
            pltpu.VMEM((seq_size * 32 + 8, LANE), F32),
            pltpu.VMEM((2, NODES, 2, COLS, LANE), BF16),
            pltpu.VMEM((2, NODES, 2, COLS, LANE), BF16),
            pltpu.VMEM((SPANS, COLS, SPAN), F32),
            dma((9,)),
            dma((2,)),
            dma,
            dma,
            dma((2,)),
            dma((2, groups)),
            dma((2,)),
            dma((2,)),
            dma((2, 2 * NODES)),
            dma((2, NODES, 2)),
            dma((4,)),
            dma((4,)),
            dma((2,)),
            dma((2,)),
            dma((NODES,)),
            dma((NODES,)),
            pltpu.VMEM((COLS, features), BF16),
            dma((SPANS,)),
        ],
        compiler_params=pltpu.CompilerParams(
            collective_id=0, has_side_effects=True, vmem_limit_bytes=60 * 1024 * 1024
        ),
        name="long_conv",
    )(
        value,
        gate_in,
        gate_out,
        skip_weight,
        spectrum,
        out_weight.reshape(QUARTERS, width // QUARTERS, features),
        *[jnp.asarray(m) for m in mats],
    )


def solution(mesh):
    placed = (
        P("seq", "chan"),
        P("seq", "chan"),
        P("seq", "chan"),
        P("chan"),
        P(None, "seq", None, "chan"),
        P("chan", None),
    )
    return jax.shard_map(
        local, mesh=mesh, in_specs=placed, out_specs=P(("seq", "chan"), None), check_vma=False
    )
```

```python
import functools
import math

import jax
import jax.numpy as jnp
import ml_dtypes
import numpy as np
from jax import lax
from jax.experimental import pallas as pl
from jax.experimental.pallas import tpu as pltpu
from jax.sharding import PartitionSpec as P

COLS = 128
LANE = 128
CH = 8
BAND = 16
GROUP = 8
NODES = 4
QUARTERS = 4
SPANS, SPAN = 4, 512
MESH = pl.DeviceIdType.MESH
F32 = jnp.float32
BF16 = jnp.bfloat16


def two_terms(matrix):
    high = matrix.astype(np.float32).astype(ml_dtypes.bfloat16)
    low = (matrix - high.astype(np.float64)).astype(np.float32).astype(ml_dtypes.bfloat16)
    return np.stack([high, low])


def constants(seq_size):
    half_rows = 8 * seq_size
    row_count = 2 * half_rows
    padded_len = row_count * COLS
    k1 = np.arange(row_count)
    a = np.arange(half_rows)
    b = np.arange(COLS)
    row = 2.0 * np.pi / row_count * (np.outer(k1, a) % row_count)
    fwd_row = np.concatenate([np.cos(row), -np.sin(row)], axis=0)
    twist = 2.0 * np.pi / padded_len * (np.outer(k1, b) % padded_len)
    turn = np.stack([np.cos(twist), np.sin(twist)]).astype(np.float32)
    col = 2.0 * np.pi / COLS * (np.outer(b, b) % COLS)
    cos, sin = np.cos(col), np.sin(col)
    fwd_col = np.block([[cos, -sin], [sin, cos]])
    inv_col = np.block([[cos, sin], [-sin, cos]])
    groups = seq_size // min(GROUP, seq_size)
    back = row.T.reshape(half_rows, groups, -1)
    inv_row = np.concatenate([np.cos(back), -np.sin(back)], axis=2) / padded_len
    inv_row = np.ascontiguousarray(inv_row.transpose(1, 0, 2))
    return two_terms(fwd_row), turn, two_terms(fwd_col), two_terms(inv_col), two_terms(inv_row)


def mm(x, y):
    return jnp.dot(x, y, preferred_element_type=F32)


def conv_kernel(
    seq_size,
    value_hbm,
    gate_in_hbm,
    gate_out_hbm,
    skip,
    spectrum,
    weight_hbm,
    fwd_row_hbm,
    turn_hbm,
    fwd_col_hbm,
    inv_col_hbm,
    inv_row_hbm,
    out,
    fwd_row,
    turn,
    fwd_col,
    inv_col,
    inv_row,
    value,
    gate_in,
    gate_out,
    spec_buf,
    weight,
    xsend,
    xrecv,
    xwide,
    xgrid,
    hwide,
    hsend,
    hrecv,
    freq,
    back,
    total,
    ysend,
    yrecv,
    ywide,
    gsend,
    grecv,
    partial,
    load_sem,
    spec_sem,
    xs,
    xr,
    hs,
    hr,
    ys,
    yr,
    gs,
    gr,
    ws,
    wr,
    es,
    er,
    cs,
    cr,
    result,
    os,
):
    me = lax.axis_index("seq")
    mc = lax.axis_index("chan")
    half_rows = 8 * seq_size
    row_count = 2 * half_rows
    width = CH * seq_size
    members = GROUP
    groups = seq_size // members
    krows = members * BAND
    px, py, low = me // 8, lax.rem(me // 2, 4), lax.rem(me, 2)
    node, core = mc // 2, lax.rem(mc, 2)
    pair_chip = me + 1 - 2 * low
    near = lax.rem(node + 3 + 2 * low, NODES)
    far = lax.rem(node + 5 - 2 * low, NODES)
    across = lax.rem(node + 2, NODES)
    mine = lax.rem(px + 2 * py, QUARTERS)
    beside = [
        lax.rem(px + 1, 4) * 8 + py * 2 + low,
        lax.rem(px + 3, 4) * 8 + py * 2 + low,
        px * 8 + lax.rem(py + 1, 4) * 2 + low,
        px * 8 + lax.rem(py + 3, 4) * 2 + low,
    ]

    def remote(src, dst, send_sem, recv_sem, seq, chan):
        return pltpu.make_async_remote_copy(
            src_ref=src,
            dst_ref=dst,
            send_sem=send_sem,
            recv_sem=recv_sem,
            device_id=(seq, chan),
            device_id_type=MESH,
        )

    mixed_loads = [
        pltpu.make_async_copy(value_hbm, value, load_sem.at[6]),
        pltpu.make_async_copy(gate_in_hbm, gate_in, load_sem.at[7]),
    ]
    weight_load = pltpu.make_async_copy(weight_hbm, weight.at[core, node], load_sem.at[8])
    loads = [
        pltpu.make_async_copy(fwd_row_hbm, fwd_row, load_sem.at[0]),
        pltpu.make_async_copy(turn_hbm, turn, load_sem.at[1]),
        pltpu.make_async_copy(fwd_col_hbm, fwd_col, load_sem.at[2]),
        pltpu.make_async_copy(inv_col_hbm, inv_col, load_sem.at[3]),
        pltpu.make_async_copy(inv_row_hbm, inv_row, load_sem.at[4]),
        pltpu.make_async_copy(gate_out_hbm, gate_out, load_sem.at[5]),
    ]
    spec_loads = [
        pltpu.make_async_copy(spectrum.at[part], spec_buf.at[part], spec_sem.at[part])
        for part in range(2)
    ]
    for copy in mixed_loads:
        copy.start()

    barrier = pltpu.get_barrier_semaphore()

    def greet(seq, chan):
        pl.semaphore_signal(barrier, inc=1, device_id=(seq, chan), device_id_type=MESH)

    def greet_seq(d, _):
        greet(lax.rem(me + d, seq_size), mc)
        return 0

    lax.fori_loop(1, seq_size, greet_seq, 0)
    greet(pair_chip, near * 2 + core)
    for step in range(1, 2 * NODES):
        greet(me, lax.rem(mc + step, 2 * NODES))

    def exchange(src_of, dst, send_sem, recv_sem):
        pltpu.make_async_copy(src_of(me), dst, recv_sem).start()

        def send(d, _):
            peer = (
                lax.rem(px + d // 8, 4) * 8
                + lax.rem(py + lax.rem(d // 2, 4), 4) * 2
                + lax.rem(low + d, 2)
            )
            remote(src_of(peer), dst, send_sem, recv_sem, peer, mc).start()
            return 0

        lax.fori_loop(1, seq_size, send, 0)

    def pass_near(step):
        block = weight.at[core, node, lax.rem(mine + step, QUARTERS)]
        sem = min(step, 1)
        return remote(block, block, ws.at[sem], wr.at[sem], pair_chip, near * 2 + core)

    def pass_pair():
        block = weight.at[core, near, mine]
        return remote(block, block, ws.at[2], wr.at[2], pair_chip, mc)

    def pass_across():
        block = weight.at[core, far, mine]
        return remote(block, block, ws.at[3], wr.at[3], pair_chip, near * 2 + core)

    def pass_beside(slot, which):
        for e, seq in enumerate(beside):
            rows = pl.ds(0, 64) if e < 2 else pl.ds((e - 2) * 32, 32)
            block = weight.at[core, which, mine, rows]
            remote(block, block, es.at[slot], er.at[slot], seq, mc).start()

    def hand_over(slot, which):
        block = weight.at[core, which]
        return remote(block, block, cs.at[slot], cr.at[slot], me, mc + 1 - 2 * core)

    def channel(dest, c):
        return (c // 4) * (width // 2) + dest * 4 + c % 4

    for copy in mixed_loads:
        copy.wait()
    for copy in [weight_load] + spec_loads + loads:
        copy.start()
    for a in range(8):
        rows = slice(a * COLS, (a + 1) * COLS)
        mixed = (gate_in[rows, :].astype(F32) * value[rows, :].astype(F32)).astype(BF16)
        xwide[a * width : (a + 1) * width, :] = mixed.astype(F32).T

    def pack_input(dest, _):
        for pair in range(CH // 2):
            rows = [
                xwide[pl.ds(channel(dest, c), 8, stride=width), :] for c in (2 * pair, 2 * pair + 1)
            ]
            xsend[dest, pair * 16 : (pair + 1) * 16, :] = jnp.concatenate(rows).astype(BF16)
        return 0

    lax.fori_loop(0, seq_size, pack_input, 0)

    weight_load.wait()
    pl.semaphore_wait(barrier, seq_size - 1 + 2 * NODES)
    pass_near(0).start()
    exchange(lambda peer: xsend.at[peer], xrecv.at[me], xs, xr)
    for step in range(1, QUARTERS):
        pass_near(step).start()
    hand_over(0, node).start()

    for part in range(2):
        spec_loads[part].wait()

        def turn_row(k, _):
            start = pl.multiple_of(k * width, width)
            hwide[pl.ds(start, width), :] = spec_buf[part, k].T
            return 0

        lax.fori_loop(0, BAND, turn_row, 0)

        def pack(dest, _):
            for c in range(CH):
                rows = hwide[pl.ds(channel(dest, c), BAND, stride=width), :]
                hsend[part, dest, c * BAND : (c + 1) * BAND, :] = rows.astype(BF16)
            return 0

        lax.fori_loop(0, seq_size, pack, 0)
        exchange(
            lambda peer: hsend.at[part, peer],
            hrecv.at[part, me],
            hs.at[part],
            hr.at[part, px],
        )
        if part == 0:
            pass_near(0).wait_recv()
            pass_pair().start()

    for copy in loads:
        copy.wait()
    pltpu.make_async_copy(xsend, xrecv, xr).wait()
    for c in range(CH):
        pair = xrecv[:, c // 2 * 16 : c // 2 * 16 + 16, :].astype(F32)
        rows = pair[:, c % 2 * 8 : c % 2 * 8 + 8, :].reshape(half_rows, LANE)
        xgrid[:, c * LANE : (c + 1) * LANE] = rows.astype(BF16)
    pass_pair().wait_recv()
    pass_across().start()
    pass_beside(0, far)

    def forward(g, _):
        rows = pl.ds(pl.multiple_of(g * krows, krows), krows)
        rows_im = pl.ds(pl.multiple_of(row_count + g * krows, krows), krows)
        cos, sin = turn[0, rows, :], turn[1, rows, :]
        for pair in range(CH // 2):
            x = xgrid[:, pair * 256 : (pair + 1) * 256]
            re = mm(fwd_row[0, rows, :], x) + mm(fwd_row[1, rows, :], x)
            im = mm(fwd_row[0, rows_im, :], x) + mm(fwd_row[1, rows_im, :], x)
            for h in range(2):
                r = re[:, h * LANE : (h + 1) * LANE]
                i = im[:, h * LANE : (h + 1) * LANE]
                turned = jnp.concatenate([r * cos + i * sin, i * cos - r * sin], axis=1)
                high = turned.astype(BF16)
                rest = (turned - high.astype(F32)).astype(BF16)
                freq[2 * pair + h, rows, :] = (
                    mm(high, fwd_col[0]) + mm(high, fwd_col[1]) + mm(rest, fwd_col[0])
                )
        return 0

    lax.fori_loop(0, groups, forward, 0)
    total[...] = jnp.zeros_like(total)

    def inverse(step, channels):
        g = lax.rem(px + groups - step, groups)
        members_at = pl.ds(pl.multiple_of(g * members, members), members)
        if 0 in channels:
            for part in range(2):
                block = hrecv.at[part, members_at]
                pltpu.make_async_copy(hsend.at[part, members_at], block, hr.at[part, g]).wait()
        rows = pl.ds(pl.multiple_of(g * krows, krows), krows)
        cos, sin = turn[0, rows, :], turn[1, rows, :]
        for c in channels:
            band = slice(c * BAND, (c + 1) * BAND)
            h_re = hrecv[0, members_at, band, :].astype(F32).reshape(krows, LANE)
            h_im = hrecv[1, members_at, band, :].astype(F32).reshape(krows, LANE)
            f_re, f_im = freq[c, rows, :LANE], freq[c, rows, LANE:]
            prod = jnp.concatenate([f_re * h_re - f_im * h_im, f_re * h_im + f_im * h_re], axis=1)
            prod = prod.astype(BF16)
            grid = mm(prod, inv_col[0]) + mm(prod, inv_col[1])
            b_re, b_im = grid[:, :LANE], grid[:, LANE:]
            lanes = slice(c * LANE, (c + 1) * LANE)
            back[:krows, lanes] = (b_re * cos - b_im * sin).astype(BF16)
            back[krows:, lanes] = (b_re * sin + b_im * cos).astype(BF16)
        for pair in range(channels[0] // 2, channels[-1] // 2 + 1):
            lanes = slice(pair * 256, (pair + 1) * 256)
            total[:, lanes] += mm(inv_row[0, g], back[:, lanes]) + mm(inv_row[1, g], back[:, lanes])

    def inverse_all(step, _):
        inverse(step, range(CH))
        return 0

    lax.fori_loop(0, groups - 1, inverse_all, 0)

    for part in range(2):
        inverse(groups - 1, range(part * 4, part * 4 + 4))
        for pair in range(2):
            halves = []
            for c in (part * 4 + 2 * pair, part * 4 + 2 * pair + 1):
                lanes = slice(c * LANE, (c + 1) * LANE)
                direct = skip[channel(me, c)] * xgrid[:, lanes].astype(F32)
                halves.append((total[:, lanes] + direct).reshape(seq_size, 8, LANE))
            rows = slice(pair * 16, (pair + 1) * 16)
            ysend[part, :, rows, :] = jnp.concatenate(halves, axis=1).astype(BF16)
        exchange(
            lambda peer: ysend.at[part, peer], yrecv.at[part, me], ys.at[part], yr.at[part]
        )

    rest = weight.at[core, near, pl.ds(0, QUARTERS - 1)]
    for part in range(2):
        pltpu.make_async_copy(ysend.at[part], yrecv.at[part], yr.at[part]).wait()
        ywide[: seq_size * 32, :] = yrecv[part].astype(F32).reshape(seq_size * 32, LANE)
        for step, h in ((1, 0), (3, 0), (1, 1), (3, 1), (2, 0), (2, 1), (0, 0), (0, 1)):
            dest = lax.rem(node + step, NODES)
            a = dest * 2 + h
            inner = ywide[pl.ds(a, width // 2, stride=8), :].T
            gate = gate_out[
                pl.ds(pl.multiple_of(a * COLS, COLS), COLS), part * LANE : (part + 1) * LANE
            ]
            gsend[part, dest, h] = (gate.astype(F32) * inner).astype(BF16)
            if step:
                remote(
                    gsend.at[part, dest, h],
                    grecv.at[part, node, core],
                    gs.at[part, step * 2 + h],
                    gr.at[part, node, core],
                    me,
                    dest * 2 + h,
                ).start()
        own = gsend.at[part, node, core]
        pltpu.make_async_copy(own, grecv.at[part, node, core], gr.at[part, node, core]).start()
        remote(
            gsend.at[part, node, 1 - core],
            grecv.at[part, node, core],
            gs.at[part, 0],
            gr.at[part, node, core],
            me,
            mc + 1 - 2 * core,
        ).start()
        if part == 0:
            pltpu.make_async_copy(rest, rest, wr.at[1]).wait()
            hand_over(1, near).start()
            pass_across().wait_recv()
            pass_beside(1, across)

    pltpu.make_async_copy(rest, rest, er.at[0]).wait()
    hand_over(2, far).start()

    def product(sources, n):
        lanes = slice(n * SPAN, (n + 1) * SPAN)
        rows = jnp.concatenate([grecv[p, w, k] for p, w in sources for k in range(2)], axis=1)
        block = jnp.concatenate(
            [
                weight[k, w, 2 * p : 2 * p + 2, :, lanes].reshape(LANE, SPAN)
                for p, w in sources
                for k in range(2)
            ]
        )
        return mm(rows, block)

    def arrive(part, which):
        for k in range(2):
            block = grecv.at[part, which, k]
            pltpu.make_async_copy(block, block, gr.at[part, which, k]).wait()

    arrive(0, node)
    arrive(1, node)
    hand_over(0, node).wait_recv()
    for n in range(SPANS):
        partial[n] = product([(0, node), (1, node)], n)
    hand_over(1, near).wait_recv()
    hand_over(2, far).wait_recv()
    arrive(0, near)
    arrive(0, far)
    for n in range(SPANS):
        partial[n] += product([(0, near), (0, far)], n)
    pltpu.make_async_copy(rest, rest, er.at[1]).wait()
    hand_over(3, across).start()
    arrive(0, across)
    hand_over(3, across).wait_recv()
    for n in range(SPANS):
        partial[n] += product([(0, across)], n)
    for which in (near, far):
        arrive(1, which)
        for n in range(SPANS):
            partial[n] += product([(1, which)], n)
    arrive(1, across)
    for n in range(SPANS):
        lanes = slice(n * SPAN, (n + 1) * SPAN)
        result[:, lanes] = (partial[n] + product([(1, across)], n)).astype(BF16)
        pltpu.make_async_copy(result.at[:, lanes], out.at[:, lanes], os.at[n]).start()
    for n in range(SPANS):
        lanes = slice(n * SPAN, (n + 1) * SPAN)
        pltpu.make_async_copy(result.at[:, lanes], out.at[:, lanes], os.at[n]).wait()

    others = pl.ds(0, seq_size - 1)
    pltpu.make_async_copy(xsend.at[others], xrecv.at[others], xs).wait()
    for part in range(2):
        pltpu.make_async_copy(hsend.at[part, others], hrecv.at[part, others], hs.at[part]).wait()
    for part in range(2):
        pltpu.make_async_copy(ysend.at[part, others], yrecv.at[part, others], ys.at[part]).wait()
        for step in [0, 2, 3, 4, 5, 6, 7]:
            pltpu.make_async_copy(
                gsend.at[0, 0, 0], grecv.at[0, 0, 0], gs.at[part, step]
            ).wait()
    for slot, which in enumerate((node, near, far, across)):
        hand_over(slot, which).wait_send()
    pass_near(0).wait_send()
    pltpu.make_async_copy(rest, rest, ws.at[1]).wait()
    pass_pair().wait_send()
    pass_across().wait_send()
    for slot in range(2):
        pltpu.make_async_copy(rest, rest, es.at[slot]).wait()


def local(value, gate_in, gate_out, skip_weight, spectrum, out_weight):
    seq_size = lax.axis_size("seq")
    half_rows = 8 * seq_size
    row_count = 2 * half_rows
    width = CH * seq_size
    features = out_weight.shape[1]
    groups = seq_size // GROUP
    krows = GROUP * BAND
    mats = constants(seq_size)
    smem = pl.BlockSpec(memory_space=pltpu.SMEM)
    hbm = pl.BlockSpec(memory_space=pl.ANY)
    dma = pltpu.SemaphoreType.DMA
    return pl.pallas_call(
        functools.partial(conv_kernel, seq_size),
        out_shape=jax.ShapeDtypeStruct((COLS, features), BF16),
        in_specs=[hbm, hbm, hbm, smem, hbm, hbm] + [hbm] * 5,
        out_specs=hbm,
        scratch_shapes=[
            *[pltpu.VMEM(m.shape, F32 if m.dtype == np.float32 else BF16) for m in mats],
            pltpu.VMEM((1024, width), BF16),
            pltpu.VMEM((1024, width), BF16),
            pltpu.VMEM((1024, width), BF16),
            pltpu.VMEM((2, BAND, COLS, width), F32),
            pltpu.VMEM((2, NODES, QUARTERS, width // QUARTERS, features), BF16),
            pltpu.VMEM((seq_size, 64, LANE), BF16),
            pltpu.VMEM((seq_size, 64, LANE), BF16),
            pltpu.VMEM((seq_size * 64 + width, LANE), F32),
            pltpu.VMEM((half_rows, CH * LANE), BF16),
            pltpu.VMEM(((BAND + 1) * width, LANE), F32),
            pltpu.VMEM((2, seq_size, CH * BAND, LANE), BF16),
            pltpu.VMEM((2, seq_size, CH * BAND, LANE), BF16),
            pltpu.VMEM((CH, row_count, 2 * LANE), F32),
            pltpu.VMEM((2 * krows, CH * LANE), BF16),
            pltpu.VMEM((half_rows, CH * LANE), F32),
            pltpu.VMEM((2, seq_size, 32, LANE), BF16),
            pltpu.VMEM((2, seq_size, 32, LANE), BF16),
            pltpu.VMEM((seq_size * 32 + 8, LANE), F32),
            pltpu.VMEM((2, NODES, 2, COLS, LANE), BF16),
            pltpu.VMEM((2, NODES, 2, COLS, LANE), BF16),
            pltpu.VMEM((SPANS, COLS, SPAN), F32),
            dma((9,)),
            dma((2,)),
            dma,
            dma,
            dma((2,)),
            dma((2, groups)),
            dma((2,)),
            dma((2,)),
            dma((2, 2 * NODES)),
            dma((2, NODES, 2)),
            dma((4,)),
            dma((4,)),
            dma((2,)),
            dma((2,)),
            dma((NODES,)),
            dma((NODES,)),
            pltpu.VMEM((COLS, features), BF16),
            dma((SPANS,)),
        ],
        compiler_params=pltpu.CompilerParams(
            collective_id=0, has_side_effects=True, vmem_limit_bytes=60 * 1024 * 1024
        ),
        name="long_conv",
    )(
        value,
        gate_in,
        gate_out,
        skip_weight,
        spectrum,
        out_weight.reshape(QUARTERS, width // QUARTERS, features),
        *[jnp.asarray(m) for m in mats],
    )


def solution(mesh):
    placed = (
        P("seq", "chan"),
        P("seq", "chan"),
        P("seq", "chan"),
        P("chan"),
        P(None, "seq", None, "chan"),
        P("chan", None),
    )
    return jax.shard_map(
        local, mesh=mesh, in_specs=placed, out_specs=P(("seq", "chan"), None), check_vma=False
    )
```
